256 devices in a mesh: line: 16 (over x_hi, y, core), out: 16 (over x_lo, z).
Axes of the slice: x: 4 (x_hi: 2, x_lo: 2; x = x_hi * 2 + x_lo), y: 4, z: 8, core: 2. Of those that a mesh axis runs over, the one named last changes fastest.
Arguments:
- injections: float32 [8, 8192], P(None, 'out'), may hold values from -6 to 6
- transfer_factors: float32 [16384, 8192], P('line', 'out'), may hold values from -0.09375 to 0.09375
- outage_factors: float32 [16384, 16384], P('line', 'out'), may hold values from -3 to 3
- line_limits: float32 [16384], P('line'), may hold values from 0.5 to 2
- outage_lines: int32 [16384], replicated, may hold values from 0 to 16383, each once
Outputs:
- injection_gradient: float32 [8, 8192], P(None, ('out', 'line'))
The draws below stay inside these ranges and needn't reach their ends.
Inputs may be any that keep to these rules, and one draw needn't show every extreme that they name: `outage_lines`: each of the 16384 lines is taken out in exactly one outage.
All inputs are finite; a program needn't handle non-finite values.
Results may differ from the reference program's by a relative error of at most 0.0001.
Values sent between devices are 32-bit elements; how exact they have to be, the bound alone decides.
No kernel may reach another device: no remote copies, remote signals or barrier semaphores. Data moves between devices by JAX's collectives and lax.ppermute only.
A program may use at most 128 MiB of HBM per device.

```python
import jax
import jax.numpy as jnp
from jax import lax

LINES = 16384
BUSES = 8192
HOURS = 8
OUTAGES = 16384


def raised(result, rng, source, target, parts, factor):
    owner, partner = [(jnp.arange(result.shape[dim]) // (result.shape[dim] // parts)).reshape([-1 if axis == dim else 1 for axis in range(result.ndim)]) for dim in (source, target)]
    chosen = jax.random.permutation(rng, parts)[partner]
    strong = (owner == chosen) | (owner == (partner + parts // 2) % parts)
    return jnp.where(strong, factor * result, result)


def steps_of(rng, shape, cuts, smallest, high):
    def one(dim, blocks):
        steps = jax.random.uniform(jax.random.fold_in(jax.random.fold_in(rng, 6), dim), (blocks,), jnp.float32, smallest / len(cuts), high / len(cuts))
        return jnp.repeat(jnp.exp(steps), shape[dim] // blocks).reshape((-1,) + (1,) * (len(shape) - dim - 1))

    loudness = one(*cuts[0])
    for cut in cuts[1:]:
        loudness = loudness * one(*cut)
    return loudness


def bell_draw(own_key, extent, spread, reach, split=(), held_as=jnp.bfloat16):
    level = steps_of(own_key, extent, split, -0.22, 0.18) if split else 1.0
    entries = jax.random.normal(own_key, extent, jnp.float32) * spread * level
    return jnp.minimum(jnp.maximum(entries, -reach), reach).astype(held_as)


def bell_draw_with(key, shape, spread, reach, cuts, heavy, kind=jnp.bfloat16):
    drawn = spread * jax.random.normal(key, shape, jnp.float32)
    if cuts:
        drawn = drawn * steps_of(key, shape, cuts, -0.22, 0.18)
    return jnp.clip(raised(drawn, jax.random.fold_in(key, 3), *heavy), -reach, reach).astype(kind)


def setup_inputs(seed: int = 0) -> dict:
    key_list = jax.random.split(jax.random.key(seed), 6)
    return {
        "injections": bell_draw(key_list[0], (HOURS, BUSES), 1.0, 6.0, ((1, 16),), jnp.float32),
        "transfer_factors": bell_draw_with(key_list[1], (LINES, BUSES), BUSES ** -0.5, 0.09375, ((0, 16), (1, 16)), (0, 1, 16, 2.0), jnp.float32),
        "outage_factors": bell_draw(key_list[2], (LINES, OUTAGES), 0.5, 3.0, ((0, 16), (1, 16)), jnp.float32),
        "line_limits": jnp.clip(0.5 + 1.5 * jax.random.uniform(key_list[3], (LINES,), jnp.float32) ** steps_of(key_list[3], (LINES,), ((0, 16),), -0.2, 0.2), 0.5, 2.0),
        "outage_lines": jax.random.permutation(key_list[4], LINES).astype(jnp.int32),
    }


SOFTNESS = 0.25


def overload_terms(factors, flow_rows, flow_out, limits, scale):
    rows, width = factors.shape
    hours = flow_rows.shape[0]
    block = min(256, rows)
    count = rows // block
    factor_blocks = factors.reshape(count, block, width)
    flow_blocks = jnp.transpose(flow_rows.reshape(hours, count, block), (1, 0, 2))
    limit_blocks = limits.reshape(count, block)

    def advance(column_total, pieces):
        factor_piece, flow_piece, limit_piece = pieces
        post = flow_piece[:, :, None] + factor_piece[None, :, :] * flow_out[:, None, :]
        bound = limit_piece[None, :, None]
        slope = (jax.nn.sigmoid((post - bound) / SOFTNESS) - jax.nn.sigmoid((-post - bound) / SOFTNESS)) * scale
        row_total = jnp.sum(slope, axis=2)
        column_total = column_total + jnp.einsum("hlk,lk->hk", slope, factor_piece, precision=lax.Precision.HIGHEST)
        return column_total, row_total

    column_total, row_blocks = lax.scan(advance, jnp.zeros((hours, width), jnp.float32), (factor_blocks, flow_blocks, limit_blocks))
    row_total = jnp.transpose(row_blocks, (1, 0, 2)).reshape(hours, rows)
    return row_total, column_total


def reference(injections, transfer_factors, outage_factors, line_limits, outage_lines):
    flows = jnp.einsum("hb,lb->hl", injections, transfer_factors, precision=lax.Precision.HIGHEST)
    flow_out = jnp.take(flows, outage_lines, axis=1)
    row_total, column_total = overload_terms(outage_factors, flows, flow_out, line_limits, 1.0 / OUTAGES)
    line_slopes = row_total.at[:, outage_lines].add(column_total)
    return jnp.einsum("hl,lb->hb", line_slopes, transfer_factors, precision=lax.Precision.HIGHEST)
```

```python
import functools

import jax
import jax.numpy as jnp
from jax import lax
from jax.experimental import pallas as pl
from jax.experimental.pallas import tpu as pltpu
from jax.sharding import PartitionSpec as P

OUTAGES = 16384
SOFTNESS = 0.25
LANES = 128
SUB = 8
VMEM = pl.BlockSpec(memory_space=pltpu.VMEM)


def params(mib):
    return pltpu.CompilerParams(vmem_limit_bytes=mib * 1024 * 1024)


def flows_kernel(injections_ref, factors_ref, out_ref):
    out_ref[...] = lax.dot_general(
        injections_ref[...],
        factors_ref[...],
        (((1,), (1,)), ((), ())),
        precision=lax.Precision.HIGHEST,
        preferred_element_type=jnp.float32,
    )


def bus_kernel(slopes_ref, factors_ref, out_ref):
    out_ref[...] = jnp.dot(
        slopes_ref[...],
        factors_ref[...],
        precision=lax.Precision.HIGHEST,
        preferred_element_type=jnp.float32,
    )


def inverse_kernel(index_ref, out_ref):
    width = index_ref.shape[1]
    lane = lax.broadcasted_iota(jnp.int32, (LANES, LANES), 1)
    row = lax.broadcasted_iota(jnp.int32, (LANES, LANES), 0)
    totals = [jnp.zeros((1, LANES), jnp.int32) for _ in range(out_ref.shape[1] // LANES)]
    for kb in range(width // LANES):
        piece = index_ref[:, kb * LANES : (kb + 1) * LANES].astype(jnp.float32)
        column = jnp.transpose(jnp.broadcast_to(piece, (LANES, LANES))).astype(jnp.int32)
        for lb in range(len(totals)):
            hit = jnp.where(column == lane + lb * LANES, row + (kb * LANES + 1), 0)
            totals[lb] = totals[lb] + jnp.sum(hit, axis=0, keepdims=True)
    for lb, total in enumerate(totals):
        out_ref[:, lb * LANES : (lb + 1) * LANES] = total - 1


def pick(values_ref, index_ref, kb):
    hours, width = values_ref.shape
    index = jnp.broadcast_to(index_ref[:, kb * LANES : (kb + 1) * LANES], (hours, LANES))
    low = jnp.bitwise_and(index, LANES - 1)
    high = jnp.right_shift(index, 7)
    result = jnp.zeros((hours, LANES), jnp.float32)
    for q in range(width // LANES):
        found = jnp.take_along_axis(values_ref[:, q * LANES : (q + 1) * LANES], low, axis=1)
        result = jnp.where(high == q, found, result)
    return result


def select_kernel(values_ref, index_ref, out_ref):
    for kb in range(out_ref.shape[1] // LANES):
        out_ref[:, kb * LANES : (kb + 1) * LANES] = pick(values_ref, index_ref, kb)


def place_kernel(values_ref, index_ref, rows_ref, out_ref):
    for kb in range(out_ref.shape[1] // LANES):
        here = slice(kb * LANES, (kb + 1) * LANES)
        out_ref[:, here] = pick(values_ref, index_ref, kb) + rows_ref[:, here]


def overload_kernel(
    factors_ref, flow_ref, out_flow_ref, limit_ref, row_ref, column_ref, up, down, wide, total, sums
):
    rows, width = factors_ref.shape
    hours = flow_ref.shape[0]
    blocks = width // LANES
    tile = 2 * SUB
    gain = 0.5 / SOFTNESS
    scale = 0.5 / OUTAGES
    pad = jnp.zeros((LANES - hours, LANES), jnp.float32)
    for lb in range(rows // LANES):
        here = slice(lb * LANES, (lb + 1) * LANES)
        flow = gain * flow_ref[:, here]
        limit = gain * limit_ref[:, here]
        up[here, :] = jnp.transpose(jnp.concatenate([flow + limit, pad], axis=0))
        down[here, :] = jnp.transpose(jnp.concatenate([flow - limit, pad], axis=0))
    for h in range(hours):
        for kb in range(blocks):
            piece = gain * out_flow_ref[h : h + 1, kb * LANES : (kb + 1) * LANES]
            wide[h * blocks + kb] = jnp.broadcast_to(piece, (SUB, LANES))
    total[...] = jnp.zeros_like(total)
    lane = lax.broadcasted_iota(jnp.int32, (SUB, LANES), 1)

    def advance(step, carry):
        start = pl.multiple_of(step * tile, tile)
        parts = range(tile // SUB)
        factor = [
            [factors_ref[pl.ds(start + r * SUB, SUB), kb * LANES : (kb + 1) * LANES] for kb in range(blocks)]
            for r in parts
        ]
        ups = [up[pl.ds(start + r * SUB, SUB), :] for r in parts]
        downs = [down[pl.ds(start + r * SUB, SUB), :] for r in parts]
        kept = [jnp.zeros((SUB, LANES), jnp.float32) for r in parts]
        for h in range(hours):
            plus = [jnp.broadcast_to(ups[r][:, h : h + 1], (SUB, LANES)) for r in parts]
            minus = [jnp.broadcast_to(downs[r][:, h : h + 1], (SUB, LANES)) for r in parts]
            across = [None for r in parts]
            for kb in range(blocks):
                out_flow = wide[h * blocks + kb]
                gathered = None
                for r in parts:
                    moved = factor[r][kb] * out_flow
                    slope = jnp.tanh(moved + plus[r]) + jnp.tanh(moved + minus[r])
                    across[r] = slope if across[r] is None else across[r] + slope
                    weighted = slope * factor[r][kb]
                    gathered = weighted if gathered is None else gathered + weighted
                total[h * blocks + kb] = total[h * blocks + kb] + gathered
            for r in parts:
                kept[r] = jnp.where(lane == h, jnp.sum(across[r], axis=1, keepdims=True), kept[r])
        for r in parts:
            sums[pl.ds(start + r * SUB, SUB), :] = kept[r]
        return carry

    lax.fori_loop(0, rows // tile, advance, 0)
    for lb in range(rows // LANES):
        here = slice(lb * LANES, (lb + 1) * LANES)
        row_ref[:, here] = scale * jnp.transpose(sums[here, :])[:hours, :]
    for h in range(hours):
        for kb in range(blocks):
            column_ref[h : h + 1, kb * LANES : (kb + 1) * LANES] = scale * jnp.sum(
                total[h * blocks + kb], axis=0, keepdims=True
            )


def call(kernel, shape, *operands, dtype=jnp.float32, mib=8, flops=0, scratch=()):
    size = sum(a.size * 4 for a in operands)
    out_shape = [jax.ShapeDtypeStruct(s, dtype) for s in shape]
    result = pl.pallas_call(
        kernel,
        out_shape=out_shape,
        in_specs=[VMEM] * len(operands),
        out_specs=[VMEM] * len(shape),
        scratch_shapes=list(scratch),
        compiler_params=params(mib),
        cost_estimate=pl.CostEstimate(flops=flops, bytes_accessed=size, transcendentals=0),
    )(*operands)
    return result[0] if len(shape) == 1 else result


def partner_sum(x, axis, partners):
    return x + lax.ppermute(x, axis, list(enumerate(partners)))


def out_steps(count):
    depth = count // 2
    steps = [[o ^ depth for o in range(count)]]
    bit = 1
    while bit < depth // 2:
        steps.append([o ^ bit for o in range(count)])
        bit *= 2
    if depth > 1:
        steps.append([(o & depth) | (depth - 1 - (o & (depth - 1))) for o in range(count)])
    return steps


def line_steps(count):
    steps = []
    bit = count // 2
    while bit:
        steps.append([i ^ bit for i in range(count)])
        bit //= 2
    return steps


def sum_over(x, axis, steps):
    for partners in steps:
        x = partner_sum(x, axis, partners)
    return x


def local(injections, transfer_factors, outage_factors, line_limits, outage_lines):
    rows, buses = transfer_factors.shape
    hours = injections.shape[0]
    width = outage_factors.shape[1]
    blocks = width // LANES
    over_out = out_steps(lax.axis_size("out"))
    over_line = line_steps(lax.axis_size("line"))
    line_start = lax.axis_index("line") * rows
    out_start = lax.axis_index("out") * width
    index = lax.dynamic_slice_in_dim(outage_lines, out_start, width, 0) - line_start
    index = index.reshape(1, width)
    limits = line_limits.reshape(1, rows)

    partial_flows = call(flows_kernel, [(hours, rows)], injections, transfer_factors, mib=16)
    inverse = call(inverse_kernel, [(1, rows)], index, dtype=jnp.int32)
    flow_rows = sum_over(partial_flows, "out", over_out)
    selected = call(select_kernel, [(hours, width)], flow_rows, index)
    flow_out = sum_over(selected, "line", over_line)
    row_part, column_part = call(
        overload_kernel,
        [(hours, rows), (hours, width)],
        outage_factors,
        flow_rows,
        flow_out,
        limits,
        mib=24,
        scratch=[
            pltpu.VMEM((rows, LANES), jnp.float32),
            pltpu.VMEM((rows, LANES), jnp.float32),
            pltpu.VMEM((hours * blocks, SUB, LANES), jnp.float32),
            pltpu.VMEM((hours * blocks, SUB, LANES), jnp.float32),
            pltpu.VMEM((rows, LANES), jnp.float32),
        ],
    )
    column_total = sum_over(column_part, "line", over_line)
    placed = call(place_kernel, [(hours, rows)], column_total, inverse, row_part)
    line_slopes = sum_over(placed, "out", over_out)
    bus_terms = call(bus_kernel, [(hours, buses)], line_slopes, transfer_factors, mib=16)
    gradient = sum_over(bus_terms, "line", over_line)
    own = buses // lax.axis_size("line")
    return lax.dynamic_slice_in_dim(gradient, lax.axis_index("line") * own, own, 1)


def solution(mesh):
    in_specs = (P(None, "out"), P("line", "out"), P("line", "out"), P("line"), P())
    out_specs = P(None, ("out", "line"))
    return jax.shard_map(local, mesh=mesh, in_specs=in_specs, out_specs=out_specs, check_vma=False)
```

```python
import functools

import jax
import jax.numpy as jnp
from jax import lax
from jax.experimental import pallas as pl
from jax.experimental.pallas import tpu as pltpu
from jax.sharding import PartitionSpec as P

OUTAGES = 16384
SOFTNESS = 0.25
LANES = 128
SUB = 8
TILES = 4
CHUNKS = 8
VMEM = pl.BlockSpec(memory_space=pltpu.VMEM)
FAR = pl.BlockSpec(memory_space=pltpu.HBM)


def params(mib):
    return pltpu.CompilerParams(vmem_limit_bytes=mib * 1024 * 1024)


def thirds(x):
    high = x.astype(jnp.bfloat16)
    rest = x - high.astype(jnp.float32)
    middle = rest.astype(jnp.bfloat16)
    return high, middle, (rest - middle.astype(jnp.float32)).astype(jnp.bfloat16)


def stacked(x):
    parts = [part.astype(jnp.float32) for part in thirds(x)]
    return jnp.concatenate(parts + [jnp.zeros_like(x)], axis=0).astype(jnp.bfloat16)


def product(parts, right, dims):
    first, second, third = (
        lax.dot_general(parts, part, dims, preferred_element_type=jnp.float32) for part in thirds(right)
    )
    h = parts.shape[0] // 4
    small = first[2 * h : 3 * h] + second[h : 2 * h] + third[:h]
    return (small + (first[h : 2 * h] + second[:h])) + first[:h]


def flows_kernel(injections_hbm, factors_hbm, out_ref, injections, factors, sems):
    chunks = sems.shape[0] - 1
    rows = factors.shape[0] // chunks
    first = pltpu.make_async_copy(injections_hbm, injections, sems.at[chunks])
    first.start()
    copies = []
    for c in range(chunks):
        here = pl.ds(c * rows, rows)
        copies.append(pltpu.make_async_copy(factors_hbm.at[here, :], factors.at[here, :], sems.at[c]))
        copies[c].start()
    first.wait()
    parts = stacked(injections[...])
    for c in range(chunks):
        copies[c].wait()
        here = slice(c * rows, (c + 1) * rows)
        out_ref[:, here] = product(parts, factors[here, :], (((1,), (1,)), ((), ())))


def bus_kernel(slopes_ref, factors_ref, out_ref):
    out_ref[...] = product(stacked(slopes_ref[...]), factors_ref[...], (((1,), (0,)), ((), ())))


def inverse_kernel(index_ref, out_ref):
    width = index_ref.shape[1]
    lane = lax.broadcasted_iota(jnp.int32, (LANES, LANES), 1)
    row = lax.broadcasted_iota(jnp.int32, (LANES, LANES), 0)
    totals = [jnp.zeros((1, LANES), jnp.int32) for _ in range(out_ref.shape[1] // LANES)]
    for kb in range(width // LANES):
        piece = index_ref[:, kb * LANES : (kb + 1) * LANES].astype(jnp.float32)
        column = jnp.transpose(jnp.broadcast_to(piece, (LANES, LANES))).astype(jnp.int32)
        for lb in range(len(totals)):
            hit = jnp.where(column == lane + lb * LANES, row + (kb * LANES + 1), 0)
            totals[lb] = totals[lb] + jnp.sum(hit, axis=0, keepdims=True)
    for lb, total in enumerate(totals):
        out_ref[:, lb * LANES : (lb + 1) * LANES] = total - 1


def pick(values_ref, index_ref, kb):
    hours, width = values_ref.shape
    index = jnp.broadcast_to(index_ref[:, kb * LANES : (kb + 1) * LANES], (hours, LANES))
    low = jnp.bitwise_and(index, LANES - 1)
    high = jnp.right_shift(index, 7)
    result = jnp.zeros((hours, LANES), jnp.float32)
    for q in range(width // LANES):
        found = jnp.take_along_axis(values_ref[:, q * LANES : (q + 1) * LANES], low, axis=1)
        result = jnp.where(high == q, found, result)
    return result


def select_kernel(values_ref, index_ref, out_ref):
    for kb in range(out_ref.shape[1] // LANES):
        out_ref[:, kb * LANES : (kb + 1) * LANES] = pick(values_ref, index_ref, kb)


def place_kernel(values_ref, index_ref, rows_ref, out_ref):
    for kb in range(out_ref.shape[1] // LANES):
        here = slice(kb * LANES, (kb + 1) * LANES)
        out_ref[:, here] = pick(values_ref, index_ref, kb) + rows_ref[:, here]


def spread_kernel(flow_ref, out_ref):
    hours, rows = flow_ref.shape
    for h in range(hours):
        for lb in range(rows // LANES):
            here = slice(lb * LANES, (lb + 1) * LANES)
            flow = (0.5 / SOFTNESS) * flow_ref[h : h + 1, here]
            out_ref[h, here, :] = jnp.transpose(jnp.broadcast_to(flow, (LANES, LANES)))


def overload_kernel(
    factors_hbm, flow_ref, limit_ref, out_flow_ref, sums_ref, column_ref, factors, sems, wide, total
):
    rows, width = factors.shape
    hours = flow_ref.shape[0]
    blocks = width // LANES
    chunks = sems.shape[0]
    chunk_rows = rows // chunks
    parts = range(TILES)
    tile = TILES * SUB

    def copy(c):
        here = pl.ds(pl.multiple_of(c * chunk_rows, chunk_rows), chunk_rows)
        return pltpu.make_async_copy(factors_hbm.at[here, :], factors.at[here, :], sems.at[c])

    for c in range(chunks):
        copy(c).start()
    for h in range(hours):
        for kb in range(blocks):
            piece = (0.5 / SOFTNESS) * out_flow_ref[h : h + 1, kb * LANES : (kb + 1) * LANES]
            wide[h * blocks + kb] = jnp.broadcast_to(piece, (SUB, LANES))
    total[...] = jnp.zeros_like(total)

    def advance(start):
        at = [pl.ds(start + r * SUB, SUB) for r in parts]
        limit = [limit_ref[at[r], :] for r in parts]
        for h in range(hours):
            flow = [flow_ref[h, at[r], :] for r in parts]
            plus = [flow[r] + limit[r] for r in parts]
            minus = [flow[r] - limit[r] for r in parts]
            across = [None for r in parts]
            for kb in range(blocks):
                out_flow = wide[h * blocks + kb]
                gathered = None
                for r in parts:
                    factor = factors[at[r], kb * LANES : (kb + 1) * LANES]
                    moved = factor * out_flow
                    slope = jnp.tanh(moved + plus[r]) + jnp.tanh(moved + minus[r])
                    across[r] = slope if across[r] is None else across[r] + slope
                    weighted = slope * factor
                    gathered = weighted if gathered is None else gathered + weighted
                total[h * blocks + kb] = total[h * blocks + kb] + gathered
            for r in parts:
                sums_ref[h, at[r], :] = across[r]

    def chunk(c, carry):
        copy(c).wait()

        def step(s, inner):
            advance(pl.multiple_of(c * chunk_rows + s * tile, tile))
            return inner

        return lax.fori_loop(0, chunk_rows // tile, step, carry)

    lax.fori_loop(0, chunks, chunk, 0)
    for h in range(hours):
        for kb in range(blocks):
            column_ref[h : h + 1, kb * LANES : (kb + 1) * LANES] = (0.5 / OUTAGES) * jnp.sum(
                total[h * blocks + kb], axis=0, keepdims=True
            )


def row_kernel(sums_ref, out_ref):
    hours, rows = out_ref.shape
    for lb in range(rows // LANES):
        here = slice(lb * LANES, (lb + 1) * LANES)
        for h in range(hours):
            out_ref[h : h + 1, here] = (0.5 / OUTAGES) * jnp.sum(
                jnp.transpose(sums_ref[h, here, :]), axis=0, keepdims=True
            )


def call(kernel, shape, *operands, dtype=jnp.float32, mib=8, far=0, scratch=()):
    size = sum(a.size * 4 for a in operands)
    out_shape = [jax.ShapeDtypeStruct(s, dtype) for s in shape]
    result = pl.pallas_call(
        kernel,
        out_shape=out_shape,
        in_specs=[FAR] * far + [VMEM] * (len(operands) - far),
        out_specs=[VMEM] * len(shape),
        scratch_shapes=list(scratch),
        compiler_params=params(mib),
        cost_estimate=pl.CostEstimate(flops=0, bytes_accessed=size, transcendentals=0),
        name=kernel.__name__,
    )(*operands)
    return result[0] if len(shape) == 1 else result


def partner_sum(x, axis, partners):
    return x + lax.ppermute(x, axis, list(enumerate(partners)))


def out_steps(count):
    depth = count // 2
    steps = [[o ^ depth for o in range(count)]]
    bit = 1
    while bit < depth // 2:
        steps.append([o ^ bit for o in range(count)])
        bit *= 2
    if depth > 1:
        steps.append([(o & depth) | (depth - 1 - (o & (depth - 1))) for o in range(count)])
    return steps


def line_steps(count):
    steps = []
    bit = count // 2
    while bit:
        steps.append([i ^ bit for i in range(count)])
        bit //= 2
    return steps


def sum_over(x, axis, steps):
    for partners in steps:
        x = partner_sum(x, axis, partners)
    return x


def local(injections, transfer_factors, outage_factors, line_limits, outage_lines):
    rows, buses = transfer_factors.shape
    hours = injections.shape[0]
    width = outage_factors.shape[1]
    blocks = width // LANES
    over_out = out_steps(lax.axis_size("out"))
    over_line = line_steps(lax.axis_size("line"))
    line_start = lax.axis_index("line") * rows
    out_start = lax.axis_index("out") * width
    index = lax.dynamic_slice_in_dim(outage_lines, out_start, width, 0) - line_start
    index = index.reshape(1, width)
    limits = jnp.broadcast_to((0.5 / SOFTNESS) * line_limits[:, None], (rows, LANES))

    partial_flows = call(
        flows_kernel,
        [(hours, rows)],
        injections,
        transfer_factors,
        mib=60,
        far=2,
        scratch=[
            pltpu.VMEM((hours, buses), jnp.float32),
            pltpu.VMEM((rows, buses), jnp.float32),
            pltpu.SemaphoreType.DMA((4 + 1,)),
        ],
    )
    flow_rows = sum_over(partial_flows, "out", over_out)
    selected = call(select_kernel, [(hours, width)], flow_rows, index)
    flow_out = selected + lax.ppermute(selected, "line", list(enumerate(over_line[0])))
    flow_spread = call(spread_kernel, [(hours, rows, LANES)], flow_rows, mib=16)
    flow_out, flow_spread, limits = lax.optimization_barrier((flow_out, flow_spread, limits))
    flow_out = sum_over(flow_out, "line", over_line[1:])
    sums, column_part = call(
        overload_kernel,
        [(hours, rows, LANES), (hours, width)],
        outage_factors,
        flow_spread,
        limits,
        flow_out,
        mib=24,
        far=1,
        scratch=[
            pltpu.VMEM((rows, width), jnp.float32),
            pltpu.SemaphoreType.DMA((CHUNKS,)),
            pltpu.VMEM((hours * blocks, SUB, LANES), jnp.float32),
            pltpu.VMEM((hours * blocks, SUB, LANES), jnp.float32),
        ],
    )
    column_total = column_part + lax.ppermute(column_part, "line", list(enumerate(over_line[0])))
    row_part = call(row_kernel, [(hours, rows)], sums, mib=16)
    column_total, row_part = lax.optimization_barrier((column_total, row_part))
    column_total = partner_sum(column_total, "line", over_line[1])
    inverse = call(inverse_kernel, [(1, rows)], index, dtype=jnp.int32)
    column_total, inverse = lax.optimization_barrier((column_total, inverse))
    column_total = sum_over(column_total, "line", over_line[2:])
    placed = call(place_kernel, [(hours, rows)], column_total, inverse, row_part)
    line_slopes = sum_over(placed, "out", over_out)
    bus_terms = call(bus_kernel, [(hours, buses)], line_slopes, transfer_factors, mib=16)
    gradient = sum_over(bus_terms, "line", over_line)
    own = buses // lax.axis_size("line")
    return lax.dynamic_slice_in_dim(gradient, lax.axis_index("line") * own, own, 1)


def solution(mesh):
    in_specs = (P(None, "out"), P("line", "out"), P("line", "out"), P("line"), P())
    out_specs = P(None, ("out", "line"))
    return jax.shard_map(local, mesh=mesh, in_specs=in_specs, out_specs=out_specs, check_vma=False)
```

```python
import functools

import jax
import jax.numpy as jnp
from jax import lax
from jax.experimental import pallas as pl
from jax.experimental.pallas import tpu as pltpu
from jax.sharding import PartitionSpec as P

OUTAGES = 16384
SOFTNESS = 0.25
LANES = 128
SUB = 8
TILES = 4
CHUNKS = 4
VMEM = pl.BlockSpec(memory_space=pltpu.VMEM)
FAR = pl.BlockSpec(memory_space=pltpu.HBM)


def params(mib):
    return pltpu.CompilerParams(vmem_limit_bytes=mib * 1024 * 1024)


def thirds(x):
    high = x.astype(jnp.bfloat16)
    rest = x - high.astype(jnp.float32)
    middle = rest.astype(jnp.bfloat16)
    return high, middle, (rest - middle.astype(jnp.float32)).astype(jnp.bfloat16)


def stacked(x):
    parts = [part.astype(jnp.float32) for part in thirds(x)]
    return jnp.concatenate(parts + [jnp.zeros_like(x)], axis=0).astype(jnp.bfloat16)


def product(parts, right, dims):
    first, second, third = (
        lax.dot_general(parts, part, dims, preferred_element_type=jnp.float32) for part in thirds(right)
    )
    h = parts.shape[0] // 4
    small = first[2 * h : 3 * h] + second[h : 2 * h] + third[:h]
    return (small + (first[h : 2 * h] + second[:h])) + first[:h]


def flows_kernel(injections_hbm, factors_hbm, out_ref, injections, factors, sems):
    chunks = sems.shape[0] - 1
    rows = factors.shape[0] // chunks
    first = pltpu.make_async_copy(injections_hbm, injections, sems.at[chunks])
    first.start()
    copies = []
    for c in range(chunks):
        here = pl.ds(c * rows, rows)
        copies.append(pltpu.make_async_copy(factors_hbm.at[here, :], factors.at[here, :], sems.at[c]))
        copies[c].start()
    first.wait()
    parts = stacked(injections[...])
    for c in range(chunks):
        copies[c].wait()
        here = slice(c * rows, (c + 1) * rows)
        out_ref[:, here] = product(parts, factors[here, :], (((1,), (1,)), ((), ())))


def bus_kernel(slopes_ref, factors_ref, out_ref):
    terms = product(stacked(slopes_ref[...]), factors_ref[...], (((1,), (0,)), ((), ())))
    pieces, hours, lanes = out_ref.shape
    own = terms.shape[1] // pieces
    out_ref[...] = jnp.zeros_like(out_ref)
    for p in range(pieces):
        out_ref[p, :, :own] = terms[:, p * own : (p + 1) * own]


def inverse_kernel(index_ref, out_ref):
    width = index_ref.shape[1]
    lane = lax.broadcasted_iota(jnp.int32, (LANES, LANES), 1)
    row = lax.broadcasted_iota(jnp.int32, (LANES, LANES), 0)
    totals = [jnp.zeros((1, LANES), jnp.int32) for _ in range(out_ref.shape[1] // LANES)]
    for kb in range(width // LANES):
        piece = index_ref[:, kb * LANES : (kb + 1) * LANES].astype(jnp.float32)
        column = jnp.transpose(jnp.broadcast_to(piece, (LANES, LANES))).astype(jnp.int32)
        for lb in range(len(totals)):
            hit = jnp.where(column == lane + lb * LANES, row + (kb * LANES + 1), 0)
            totals[lb] = totals[lb] + jnp.sum(hit, axis=0, keepdims=True)
    for lb, total in enumerate(totals):
        out_ref[:, lb * LANES : (lb + 1) * LANES] = total - 1


def pick(values_ref, index_ref, kb):
    hours, width = values_ref.shape
    index = jnp.broadcast_to(index_ref[:, kb * LANES : (kb + 1) * LANES], (hours, LANES))
    low = jnp.bitwise_and(index, LANES - 1)
    high = jnp.right_shift(index, 7)
    result = jnp.zeros((hours, LANES), jnp.float32)
    for q in range(width // LANES):
        found = jnp.take_along_axis(values_ref[:, q * LANES : (q + 1) * LANES], low, axis=1)
        result = jnp.where(high == q, found, result)
    return result


def select_kernel(values_ref, index_ref, out_ref):
    for kb in range(out_ref.shape[1] // LANES):
        out_ref[:, kb * LANES : (kb + 1) * LANES] = pick(values_ref, index_ref, kb)


def place_kernel(values_ref, index_ref, rows_ref, out_ref):
    for kb in range(out_ref.shape[1] // LANES):
        here = slice(kb * LANES, (kb + 1) * LANES)
        out_ref[:, here] = pick(values_ref, index_ref, kb) + rows_ref[:, here]


def spread_kernel(flow_ref, out_ref):
    hours, rows = flow_ref.shape
    for h in range(hours):
        for lb in range(rows // LANES):
            here = slice(lb * LANES, (lb + 1) * LANES)
            flow = (0.5 / SOFTNESS) * flow_ref[h : h + 1, here]
            out_ref[h, here, :] = jnp.transpose(jnp.broadcast_to(flow, (LANES, LANES)))


def overload_kernel(
    factors_ref, flow_ref, limit_ref, out_flow_ref, sums_ref, column_ref, wide, total
):
    rows, width = factors_ref.shape
    hours = flow_ref.shape[0]
    blocks = width // LANES
    parts = range(TILES)
    tile = TILES * SUB
    for h in range(hours):
        for kb in range(blocks):
            piece = (0.5 / SOFTNESS) * out_flow_ref[h : h + 1, kb * LANES : (kb + 1) * LANES]
            wide[h * blocks + kb] = jnp.broadcast_to(piece, (SUB, LANES))
    total[...] = jnp.zeros_like(total)

    def advance(step, carry):
        start = pl.multiple_of(step * tile, tile)
        at = [pl.ds(start + r * SUB, SUB) for r in parts]
        limit = [limit_ref[at[r], :] for r in parts]
        for h in range(hours):
            flow = [flow_ref[h, at[r], :] for r in parts]
            plus = [flow[r] + limit[r] for r in parts]
            minus = [flow[r] - limit[r] for r in parts]
            across = [None for r in parts]
            for kb in range(blocks):
                out_flow = wide[h * blocks + kb]
                gathered = None
                for r in parts:
                    factor = factors_ref[at[r], kb * LANES : (kb + 1) * LANES]
                    moved = factor * out_flow
                    slope = jnp.tanh(moved + plus[r]) + jnp.tanh(moved + minus[r])
                    across[r] = slope if across[r] is None else across[r] + slope
                    weighted = slope * factor
                    gathered = weighted if gathered is None else gathered + weighted
                total[h * blocks + kb] = total[h * blocks + kb] + gathered
            for r in parts:
                sums_ref[h, at[r], :] = across[r]
        return carry

    lax.fori_loop(0, rows // tile, advance, 0)
    for h in range(hours):
        for kb in range(blocks):
            column_ref[h : h + 1, kb * LANES : (kb + 1) * LANES] = (0.5 / OUTAGES) * jnp.sum(
                total[h * blocks + kb], axis=0, keepdims=True
            )


def row_kernel(sums_ref, out_ref):
    hours, rows = out_ref.shape
    for lb in range(rows // LANES):
        here = slice(lb * LANES, (lb + 1) * LANES)
        for h in range(hours):
            out_ref[h : h + 1, here] = (0.5 / OUTAGES) * jnp.sum(
                jnp.transpose(sums_ref[h, here, :]), axis=0, keepdims=True
            )


def call(kernel, shape, *operands, dtype=jnp.float32, mib=8, far=0, scratch=()):
    size = sum(a.size * 4 for a in operands)
    out_shape = [jax.ShapeDtypeStruct(s, dtype) for s in shape]
    result = pl.pallas_call(
        kernel,
        out_shape=out_shape,
        in_specs=[FAR] * far + [VMEM] * (len(operands) - far),
        out_specs=[VMEM] * len(shape),
        scratch_shapes=list(scratch),
        compiler_params=params(mib),
        cost_estimate=pl.CostEstimate(flops=0, bytes_accessed=size, transcendentals=0),
        name=kernel.__name__,
    )(*operands)
    return result[0] if len(shape) == 1 else result


def received(x, axis, partners):
    return lax.ppermute(x, axis, list(enumerate(partners)))


def group_sum(x, axis, groups):
    copies = jnp.broadcast_to(x, (len(groups[0]),) + x.shape)
    return lax.all_to_all(copies, axis, 0, 0, axis_index_groups=groups, tiled=True).sum(0)


BWD_LINE = "a2a"
BWD_OUT = "rd"
FIN = "a2a"


def out_sum(x):
    count = lax.axis_size("out")
    depth = count // 2
    x = x + received(x, "out", [o ^ depth for o in range(count)])
    return group_sum(x, "out", [[g * depth + z for z in range(depth)] for g in range(2)])


def line_pair_steps(count):
    half = count // 2
    steps = [[i ^ half for i in range(count)]]
    if half > 2:
        steps.append([i ^ (half - 2) for i in range(count)])
    bit = 2
    while bit < half // 2:
        steps.append([i ^ bit for i in range(count)])
        bit *= 2
    return steps + [cores(count)]


def out_pair_steps(count):
    depth = count // 2
    steps = [[o ^ depth for o in range(count)]]
    bit = 1
    while bit < depth // 2:
        steps.append([o ^ bit for o in range(count)])
        bit *= 2
    if depth > 1:
        steps.append([(o & depth) | (depth - 1 - (o & (depth - 1))) for o in range(count)])
    return steps


def cores(count):
    return [i ^ 1 for i in range(count)]


def chips(count):
    return [[i for i in range(count) if i % 2 == core] for core in range(2)]


def local(injections, transfer_factors, outage_factors, line_limits, outage_lines):
    rows, buses = transfer_factors.shape
    hours = injections.shape[0]
    width = outage_factors.shape[1]
    blocks = width // LANES
    lines = lax.axis_size("line")
    line_start = lax.axis_index("line") * rows
    out_start = lax.axis_index("out") * width
    index = lax.dynamic_slice_in_dim(outage_lines, out_start, width, 0) - line_start
    index = index.reshape(1, width)
    limits = jnp.broadcast_to((0.5 / SOFTNESS) * line_limits[:, None], (rows, LANES))

    partial_flows = call(
        flows_kernel,
        [(hours, rows)],
        injections,
        transfer_factors,
        mib=60,
        far=2,
        scratch=[
            pltpu.VMEM((hours, buses), jnp.float32),
            pltpu.VMEM((rows, buses), jnp.float32),
            pltpu.SemaphoreType.DMA((CHUNKS + 1,)),
        ],
    )
    inverse = call(inverse_kernel, [(1, rows)], index, dtype=jnp.int32)
    flow_rows = partial_flows
    for partners in out_pair_steps(lax.axis_size("out")):
        flow_rows = flow_rows + received(flow_rows, "out", partners)
    flow_rows, inverse, limits = lax.optimization_barrier((flow_rows, inverse, limits))
    selected = call(select_kernel, [(hours, width)], flow_rows, index)
    first, *others = line_pair_steps(lines)
    flow_out = selected + received(selected, "line", first)
    flow_spread = call(spread_kernel, [(hours, rows, LANES)], flow_rows, mib=16)
    flow_out, flow_spread = lax.optimization_barrier((flow_out, flow_spread))
    for partners in others:
        flow_out = flow_out + received(flow_out, "line", partners)
    sums, column_part = call(
        overload_kernel,
        [(hours, rows, LANES), (hours, width)],
        outage_factors,
        flow_spread,
        limits,
        flow_out,
        mib=24,
        scratch=[
            pltpu.VMEM((hours * blocks, SUB, LANES), jnp.float32),
            pltpu.VMEM((hours * blocks, SUB, LANES), jnp.float32),
        ],
    )
    if BWD_LINE == "a2a":
        column_total = column_part + received(column_part, "line", cores(lines))
    else:
        column_total = column_part + received(column_part, "line", first)
    row_part = call(row_kernel, [(hours, rows)], sums, mib=16)
    column_total, row_part = lax.optimization_barrier((column_total, row_part))
    if BWD_LINE == "a2a":
        column_total = group_sum(column_total, "line", chips(lines))
    else:
        for partners in others:
            column_total = column_total + received(column_total, "line", partners)
    placed = call(place_kernel, [(hours, rows)], column_total, inverse, row_part)
    if BWD_OUT == "a2a":
        line_slopes = out_sum(placed)
    else:
        line_slopes = placed
        for partners in out_pair_steps(lax.axis_size("out")):
            line_slopes = line_slopes + received(line_slopes, "out", partners)
    pieces = call(bus_kernel, [(lines, hours, LANES)], line_slopes, transfer_factors, mib=16)
    if FIN == "a2a":
        gradient = lax.all_to_all(pieces, "line", 0, 0, tiled=True).sum(0)
    else:
        for partners in line_pair_steps(lines):
            pieces = pieces + received(pieces, "line", partners)
        gradient = lax.dynamic_index_in_dim(pieces, lax.axis_index("line"), 0, keepdims=False)
    return gradient[:, : buses // lines]


def solution(mesh):
    in_specs = (P(None, "out"), P("line", "out"), P("line", "out"), P("line"), P())
    out_specs = P(None, ("out", "line"))
    return jax.shard_map(local, mesh=mesh, in_specs=in_specs, out_specs=out_specs, check_vma=False)
```

```python
import functools

import jax
import jax.numpy as jnp
from jax import lax
from jax.experimental import pallas as pl
from jax.experimental.pallas import tpu as pltpu
from jax.sharding import PartitionSpec as P

OUTAGES = 16384
SOFTNESS = 0.25
LANES = 128
SUB = 8
TILES = 4
CHUNKS = 4
VMEM = pl.BlockSpec(memory_space=pltpu.VMEM)
FAR = pl.BlockSpec(memory_space=pltpu.HBM)


def params(mib):
    return pltpu.CompilerParams(vmem_limit_bytes=mib * 1024 * 1024)


def thirds(x):
    high = x.astype(jnp.bfloat16)
    rest = x - high.astype(jnp.float32)
    middle = rest.astype(jnp.bfloat16)
    return high, middle, (rest - middle.astype(jnp.float32)).astype(jnp.bfloat16)


def stacked(x):
    parts = [part.astype(jnp.float32) for part in thirds(x)]
    return jnp.concatenate(parts + [jnp.zeros_like(x)], axis=0).astype(jnp.bfloat16)


def product(parts, right, dims):
    first, second, third = (
        lax.dot_general(parts, part, dims, preferred_element_type=jnp.float32) for part in thirds(right)
    )
    h = parts.shape[0] // 4
    small = first[2 * h : 3 * h] + second[h : 2 * h] + third[:h]
    return (small + (first[h : 2 * h] + second[:h])) + first[:h]


def flows_kernel(injections_hbm, factors_hbm, out_ref, injections, factors, sems):
    chunks = sems.shape[0] - 1
    rows = factors.shape[0] // chunks
    first = pltpu.make_async_copy(injections_hbm, injections, sems.at[chunks])
    first.start()
    copies = []
    for c in range(chunks):
        here = pl.ds(c * rows, rows)
        copies.append(pltpu.make_async_copy(factors_hbm.at[here, :], factors.at[here, :], sems.at[c]))
        copies[c].start()
    first.wait()
    parts = stacked(injections[...])
    for c in range(chunks):
        copies[c].wait()
        here = slice(c * rows, (c + 1) * rows)
        out_ref[:, here] = product(parts, factors[here, :], (((1,), (1,)), ((), ())))


def bus_kernel(slopes_ref, factors_ref, out_ref):
    terms = product(stacked(slopes_ref[...]), factors_ref[...], (((1,), (0,)), ((), ())))
    pieces, hours, lanes = out_ref.shape
    own = terms.shape[1] // pieces
    out_ref[...] = jnp.zeros_like(out_ref)
    for p in range(pieces):
        out_ref[p, :, :own] = terms[:, p * own : (p + 1) * own]


def inverse_kernel(index_ref, out_ref):
    width = index_ref.shape[1]
    lane = lax.broadcasted_iota(jnp.int32, (LANES, LANES), 1)
    row = lax.broadcasted_iota(jnp.int32, (LANES, LANES), 0)
    totals = [jnp.zeros((1, LANES), jnp.int32) for _ in range(out_ref.shape[1] // LANES)]
    for kb in range(width // LANES):
        piece = index_ref[:, kb * LANES : (kb + 1) * LANES].astype(jnp.float32)
        column = jnp.transpose(jnp.broadcast_to(piece, (LANES, LANES))).astype(jnp.int32)
        for lb in range(len(totals)):
            hit = jnp.where(column == lane + lb * LANES, row + (kb * LANES + 1), 0)
            totals[lb] = totals[lb] + jnp.sum(hit, axis=0, keepdims=True)
    for lb, total in enumerate(totals):
        out_ref[:, lb * LANES : (lb + 1) * LANES] = total - 1


def pick(values_ref, index_ref, kb):
    hours, width = values_ref.shape
    index = jnp.broadcast_to(index_ref[:, kb * LANES : (kb + 1) * LANES], (hours, LANES))
    low = jnp.bitwise_and(index, LANES - 1)
    high = jnp.right_shift(index, 7)
    result = jnp.zeros((hours, LANES), jnp.float32)
    for q in range(width // LANES):
        found = jnp.take_along_axis(values_ref[:, q * LANES : (q + 1) * LANES], low, axis=1)
        result = jnp.where(high == q, found, result)
    return result


def select_kernel(values_ref, index_ref, out_ref):
    for kb in range(out_ref.shape[1] // LANES):
        out_ref[:, kb * LANES : (kb + 1) * LANES] = pick(values_ref, index_ref, kb)


def place_kernel(values_ref, index_ref, rows_ref, out_ref):
    for kb in range(out_ref.shape[1] // LANES):
        here = slice(kb * LANES, (kb + 1) * LANES)
        out_ref[:, here] = pick(values_ref, index_ref, kb) + rows_ref[:, here]


def spread_kernel(flow_ref, out_ref):
    hours, rows = flow_ref.shape
    for h in range(hours):
        for lb in range(rows // LANES):
            here = slice(lb * LANES, (lb + 1) * LANES)
            flow = (0.5 / SOFTNESS) * flow_ref[h : h + 1, here]
            out_ref[h, here, :] = jnp.transpose(jnp.broadcast_to(flow, (LANES, LANES)))


def overload_kernel(
    factors_ref, flow_ref, limit_ref, out_flow_ref, sums_ref, column_ref, wide, total
):
    rows, width = factors_ref.shape
    hours = flow_ref.shape[0]
    blocks = width // LANES
    parts = range(TILES)
    tile = TILES * SUB
    for h in range(hours):
        for kb in range(blocks):
            piece = (0.5 / SOFTNESS) * out_flow_ref[h : h + 1, kb * LANES : (kb + 1) * LANES]
            wide[h * blocks + kb] = jnp.broadcast_to(piece, (SUB, LANES))
    total[...] = jnp.zeros_like(total)

    def advance(step, carry):
        start = pl.multiple_of(step * tile, tile)
        at = [pl.ds(start + r * SUB, SUB) for r in parts]
        limit = [limit_ref[at[r], :] for r in parts]
        for h in range(hours):
            flow = [flow_ref[h, at[r], :] for r in parts]
            plus = [flow[r] + limit[r] for r in parts]
            minus = [flow[r] - limit[r] for r in parts]
            across = [None for r in parts]
            for kb in range(blocks):
                out_flow = wide[h * blocks + kb]
                gathered = None
                for r in parts:
                    factor = factors_ref[at[r], kb * LANES : (kb + 1) * LANES]
                    moved = factor * out_flow
                    slope = jnp.tanh(moved + plus[r]) + jnp.tanh(moved + minus[r])
                    across[r] = slope if across[r] is None else across[r] + slope
                    weighted = slope * factor
                    gathered = weighted if gathered is None else gathered + weighted
                total[h * blocks + kb] = total[h * blocks + kb] + gathered
            for r in parts:
                sums_ref[h, at[r], :] = across[r]
        return carry

    lax.fori_loop(0, rows // tile, advance, 0)
    for h in range(hours):
        for kb in range(blocks):
            column_ref[h : h + 1, kb * LANES : (kb + 1) * LANES] = (0.5 / OUTAGES) * jnp.sum(
                total[h * blocks + kb], axis=0, keepdims=True
            )


def row_kernel(sums_ref, out_ref):
    hours, rows = out_ref.shape
    for lb in range(rows // LANES):
        here = slice(lb * LANES, (lb + 1) * LANES)
        for h in range(hours):
            out_ref[h : h + 1, here] = (0.5 / OUTAGES) * jnp.sum(
                jnp.transpose(sums_ref[h, here, :]), axis=0, keepdims=True
            )


def call(kernel, shape, *operands, dtype=jnp.float32, mib=8, far=0, scratch=()):
    size = sum(a.size * 4 for a in operands)
    out_shape = [jax.ShapeDtypeStruct(s, dtype) for s in shape]
    result = pl.pallas_call(
        kernel,
        out_shape=out_shape,
        in_specs=[FAR] * far + [VMEM] * (len(operands) - far),
        out_specs=[VMEM] * len(shape),
        scratch_shapes=list(scratch),
        compiler_params=params(mib),
        cost_estimate=pl.CostEstimate(flops=0, bytes_accessed=size, transcendentals=0),
        name=kernel.__name__,
    )(*operands)
    return result[0] if len(shape) == 1 else result


def pairs_over(dims, moves):
    lines, outs = dims
    pairs = []
    for i in range(lines):
        for o in range(outs):
            to_line, to_out = moves(i, o)
            pairs.append((i * outs + o, to_line * outs + to_out))
    return pairs


def out_moves(outs):
    depth = outs // 2
    moves = [lambda i, o: (i, o ^ depth)]
    bit = 1
    while bit < depth // 2:
        moves.append(lambda i, o, bit=bit: (i, o ^ bit))
        bit *= 2
    if depth > 1:
        moves.append(lambda i, o: (i, (o & depth) | (depth - 1 - (o & (depth - 1)))))
    return moves


def line_moves(lines):
    half = lines // 2
    moves = [lambda i, o: (i ^ half ^ 1, o)]
    if half > 2:
        moves.append(lambda i, o: (i ^ (half - 2) ^ 1, o))
    bit = 2
    while bit < half // 2:
        moves.append(lambda i, o, bit=bit: (i ^ bit ^ 1, o))
        bit *= 2
    return moves


def local(injections, transfer_factors, outage_factors, line_limits, outage_lines):
    rows, buses = transfer_factors.shape
    hours = injections.shape[0]
    width = outage_factors.shape[1]
    blocks = width // LANES
    lines, outs = lax.axis_size("line"), lax.axis_size("out")
    line = lax.axis_index("line")
    out_start = lax.axis_index("out") * width
    index = lax.dynamic_slice_in_dim(outage_lines, out_start, width, 0) - line * rows
    index = index.reshape(1, width)
    limits = jnp.broadcast_to((0.5 / SOFTNESS) * line_limits[:, None], (rows, LANES))

    def add_move(x, move):
        return x + lax.ppermute(x, ("line", "out"), pairs_over((lines, outs), move))

    def other_core(x):
        return lax.ppermute(x, "line", [(i, i ^ 1) for i in range(lines)])

    over_out, over_line = out_moves(outs), line_moves(lines)
    flows = call(
        flows_kernel,
        [(hours, rows)],
        injections,
        transfer_factors,
        mib=60,
        far=2,
        scratch=[
            pltpu.VMEM((hours, buses), jnp.float32),
            pltpu.VMEM((rows, buses), jnp.float32),
            pltpu.SemaphoreType.DMA((CHUNKS + 1,)),
        ],
    )
    inverse = call(inverse_kernel, [(1, rows)], index, dtype=jnp.int32)
    for move in over_out:
        flows = add_move(flows, move)
    flows, inverse, limits = lax.optimization_barrier((flows, inverse, limits))
    flow_out = call(select_kernel, [(hours, width)], flows, index)
    flow_out = flow_out + other_core(flow_out)
    flow_spread = call(spread_kernel, [(hours, rows, LANES)], flows, mib=16)
    flow_out, flow_spread = lax.optimization_barrier((flow_out, flow_spread))
    for move in over_line:
        flow_out = add_move(flow_out, move)
    sums, column_part = call(
        overload_kernel,
        [(hours, rows, LANES), (hours, width)],
        outage_factors,
        flow_spread,
        limits,
        flow_out,
        mib=24,
        scratch=[
            pltpu.VMEM((hours * blocks, SUB, LANES), jnp.float32),
            pltpu.VMEM((hours * blocks, SUB, LANES), jnp.float32),
        ],
    )
    column_total = column_part + other_core(column_part)
    row_part = call(row_kernel, [(hours, rows)], sums, mib=16)
    column_total, row_part = lax.optimization_barrier((column_total, row_part))
    copies = jnp.broadcast_to(column_total, (lines // 2,) + column_total.shape)
    column_total = lax.all_to_all(
        copies, "line", 0, 0, axis_index_groups=[list(range(c, lines, 2)) for c in range(2)], tiled=True
    ).sum(0)
    slopes = call(place_kernel, [(hours, rows)], column_total, inverse, row_part)
    for move in over_out:
        slopes = add_move(slopes, move)
    pieces = call(bus_kernel, [(lines, hours, LANES)], slopes, transfer_factors, mib=16)
    gradient = lax.all_to_all(pieces, "line", 0, 0, tiled=True).sum(0)
    return gradient[:, : buses // lines]


def solution(mesh):
    in_specs = (P(None, "out"), P("line", "out"), P("line", "out"), P("line"), P())
    out_specs = P(None, ("out", "line"))
    return jax.shard_map(local, mesh=mesh, in_specs=in_specs, out_specs=out_specs, check_vma=False)
```

```python
import functools

import jax
import jax.numpy as jnp
from jax import lax
from jax.experimental import pallas as pl
from jax.experimental.pallas import tpu as pltpu
from jax.sharding import PartitionSpec as P

OUTAGES = 16384
SOFTNESS = 0.25
LANES = 128
SUB = 8
TILES = 4
CHUNKS = 2
VMEM = pl.BlockSpec(memory_space=pltpu.VMEM)
FAR = pl.BlockSpec(memory_space=pltpu.HBM)


def params(mib):
    return pltpu.CompilerParams(vmem_limit_bytes=mib * 1024 * 1024)


def thirds(x):
    high = x.astype(jnp.bfloat16)
    rest = x - high.astype(jnp.float32)
    middle = rest.astype(jnp.bfloat16)
    return high, middle, (rest - middle.astype(jnp.float32)).astype(jnp.bfloat16)


def stacked(x):
    parts = [part.astype(jnp.float32) for part in thirds(x)]
    return jnp.concatenate(parts + [jnp.zeros_like(x)], axis=0).astype(jnp.bfloat16)


def product(parts, right, dims):
    first, second, third = (
        lax.dot_general(parts, part, dims, preferred_element_type=jnp.float32) for part in right
    )
    h = parts.shape[0] // 4
    small = first[2 * h : 3 * h] + second[h : 2 * h] + third[:h]
    return (small + (first[h : 2 * h] + second[:h])) + first[:h]


def flows_kernel(injections_hbm, factors_hbm, out_ref, injections, factors, sems):
    chunks = sems.shape[0] - 1
    rows = factors.shape[0] // chunks
    first = pltpu.make_async_copy(injections_hbm, injections, sems.at[chunks])
    first.start()
    copies = []
    for c in range(chunks):
        here = pl.ds(c * rows, rows)
        copies.append(pltpu.make_async_copy(factors_hbm.at[here, :], factors.at[here, :], sems.at[c]))
        copies[c].start()
    first.wait()
    parts = stacked(injections[...])
    for c in range(chunks):
        copies[c].wait()
        here = slice(c * rows, (c + 1) * rows)
        out_ref[:, here] = product(parts, thirds(factors[here, :]), (((1,), (1,)), ((), ())))


def copy_kernel(x_ref, out_ref):
    out_ref[...] = x_ref[...]


def thirds_kernel(x_ref, out_ref):
    for part, third in enumerate(thirds(x_ref[...])):
        out_ref[part] = third


def bus_kernel(slopes_ref, factors_ref, out_ref):
    parts = [factors_ref[part] for part in range(factors_ref.shape[0])]
    terms = product(stacked(slopes_ref[...]), parts, (((1,), (0,)), ((), ())))
    pieces, hours, lanes = out_ref.shape
    own = terms.shape[1] // pieces
    out_ref[...] = jnp.zeros_like(out_ref)
    for p in range(pieces):
        out_ref[p, :, :own] = terms[:, p * own : (p + 1) * own]


def inverse_kernel(index_ref, out_ref):
    width = index_ref.shape[1]
    lane = lax.broadcasted_iota(jnp.int32, (LANES, LANES), 1)
    row = lax.broadcasted_iota(jnp.int32, (LANES, LANES), 0)
    totals = [jnp.zeros((1, LANES), jnp.int32) for _ in range(out_ref.shape[1] // LANES)]
    for kb in range(width // LANES):
        piece = index_ref[:, kb * LANES : (kb + 1) * LANES].astype(jnp.float32)
        column = jnp.transpose(jnp.broadcast_to(piece, (LANES, LANES))).astype(jnp.int32)
        for lb in range(len(totals)):
            hit = jnp.where(column == lane + lb * LANES, row + (kb * LANES + 1), 0)
            totals[lb] = totals[lb] + jnp.sum(hit, axis=0, keepdims=True)
    for lb, total in enumerate(totals):
        out_ref[:, lb * LANES : (lb + 1) * LANES] = total - 1


def pick(values_ref, index_ref, kb):
    hours, width = values_ref.shape
    index = jnp.broadcast_to(index_ref[:, kb * LANES : (kb + 1) * LANES], (hours, LANES))
    low = jnp.bitwise_and(index, LANES - 1)
    high = jnp.right_shift(index, 7)
    result = jnp.zeros((hours, LANES), jnp.float32)
    for q in range(width // LANES):
        found = jnp.take_along_axis(values_ref[:, q * LANES : (q + 1) * LANES], low, axis=1)
        result = jnp.where(high == q, found, result)
    return result


def select_kernel(values_ref, index_ref, out_ref):
    for kb in range(out_ref.shape[1] // LANES):
        out_ref[:, kb * LANES : (kb + 1) * LANES] = pick(values_ref, index_ref, kb)


def place_kernel(values_ref, index_ref, rows_ref, out_ref):
    for kb in range(out_ref.shape[1] // LANES):
        here = slice(kb * LANES, (kb + 1) * LANES)
        out_ref[:, here] = pick(values_ref, index_ref, kb) + rows_ref[:, here]


def spread_kernel(flow_ref, out_ref):
    hours, rows = flow_ref.shape
    for h in range(hours):
        for lb in range(rows // LANES):
            here = slice(lb * LANES, (lb + 1) * LANES)
            flow = (0.5 / SOFTNESS) * flow_ref[h : h + 1, here]
            out_ref[h, here, :] = jnp.transpose(jnp.broadcast_to(flow, (LANES, LANES)))


def overload_kernel(
    factors_ref, flow_ref, limit_ref, out_flow_ref, sums_ref, column_ref, wide, total
):
    rows, width = factors_ref.shape
    hours = flow_ref.shape[0]
    blocks = width // LANES
    parts = range(TILES)
    tile = TILES * SUB
    for h in range(hours):
        for kb in range(blocks):
            piece = (0.5 / SOFTNESS) * out_flow_ref[h : h + 1, kb * LANES : (kb + 1) * LANES]
            wide[h * blocks + kb] = jnp.broadcast_to(piece, (SUB, LANES))
    total[...] = jnp.zeros_like(total)

    def advance(step, carry):
        start = pl.multiple_of(step * tile, tile)
        at = [pl.ds(start + r * SUB, SUB) for r in parts]
        limit = [limit_ref[at[r], :] for r in parts]
        for h in range(hours):
            flow = [flow_ref[h, at[r], :] for r in parts]
            plus = [flow[r] + limit[r] for r in parts]
            minus = [flow[r] - limit[r] for r in parts]
            across = [None for r in parts]
            for kb in range(blocks):
                out_flow = wide[h * blocks + kb]
                gathered = None
                for r in parts:
                    factor = factors_ref[at[r], kb * LANES : (kb + 1) * LANES]
                    moved = factor * out_flow
                    slope = jnp.tanh(moved + plus[r]) + jnp.tanh(moved + minus[r])
                    across[r] = slope if across[r] is None else across[r] + slope
                    weighted = slope * factor
                    gathered = weighted if gathered is None else gathered + weighted
                total[h * blocks + kb] = total[h * blocks + kb] + gathered
            for r in parts:
                sums_ref[h, at[r], :] = across[r]
        return carry

    lax.fori_loop(0, rows // tile, advance, 0)
    for h in range(hours):
        for kb in range(blocks):
            column_ref[h : h + 1, kb * LANES : (kb + 1) * LANES] = (0.5 / OUTAGES) * jnp.sum(
                total[h * blocks + kb], axis=0, keepdims=True
            )


def row_kernel(sums_ref, out_ref):
    hours, rows = out_ref.shape
    for lb in range(rows // LANES):
        here = slice(lb * LANES, (lb + 1) * LANES)
        for h in range(hours):
            out_ref[h : h + 1, here] = (0.5 / OUTAGES) * jnp.sum(
                jnp.transpose(sums_ref[h, here, :]), axis=0, keepdims=True
            )


def call(kernel, shape, *operands, dtype=jnp.float32, mib=8, far=0, scratch=()):
    size = sum(a.size * 4 for a in operands)
    out_shape = [jax.ShapeDtypeStruct(s, dtype) for s in shape]
    result = pl.pallas_call(
        kernel,
        out_shape=out_shape,
        in_specs=[FAR] * far + [VMEM] * (len(operands) - far),
        out_specs=[VMEM] * len(shape),
        scratch_shapes=list(scratch),
        compiler_params=params(mib),
        cost_estimate=pl.CostEstimate(flops=0, bytes_accessed=size, transcendentals=0),
        name=kernel.__name__,
    )(*operands)
    return result[0] if len(shape) == 1 else result


def pairs_over(dims, moves):
    lines, outs = dims
    pairs = []
    for i in range(lines):
        for o in range(outs):
            to_line, to_out = moves(i, o)
            pairs.append((i * outs + o, to_line * outs + to_out))
    return pairs


def out_moves(outs):
    depth = outs // 2
    moves = [lambda i, o: (i, o ^ depth)]
    bit = 1
    while bit < depth // 2:
        moves.append(lambda i, o, bit=bit: (i, o ^ bit))
        bit *= 2
    if depth > 1:
        moves.append(lambda i, o: (i, (o & depth) | (depth - 1 - (o & (depth - 1)))))
    return moves


def line_moves(lines):
    half = lines // 2
    moves = [lambda i, o: (i ^ half ^ 1, o)]
    if half > 2:
        moves.append(lambda i, o: (i ^ (half - 2) ^ 1, o))
    bit = 2
    while bit < half // 2:
        moves.append(lambda i, o, bit=bit: (i ^ bit ^ 1, o))
        bit *= 2
    return moves


def local(injections, transfer_factors, outage_factors, line_limits, outage_lines):
    rows, buses = transfer_factors.shape
    hours = injections.shape[0]
    width = outage_factors.shape[1]
    blocks = width // LANES
    lines, outs = lax.axis_size("line"), lax.axis_size("out")
    line = lax.axis_index("line")
    out_start = lax.axis_index("out") * width
    index = lax.dynamic_slice_in_dim(outage_lines, out_start, width, 0) - line * rows
    index = index.reshape(1, width)
    limits = jnp.broadcast_to((0.5 / SOFTNESS) * line_limits[:, None], (rows, LANES))

    def moved(x, move):
        return lax.ppermute(x, ("line", "out"), pairs_over((lines, outs), move))

    def add_move(x, move):
        return x + moved(x, move)

    def other_core(x):
        return lax.ppermute(x, "line", [(i, i ^ 1) for i in range(lines)])

    over_out, over_line = out_moves(outs), line_moves(lines)
    flows = call(
        flows_kernel,
        [(hours, rows)],
        injections,
        transfer_factors,
        mib=60,
        far=2,
        scratch=[
            pltpu.VMEM((hours, buses), jnp.float32),
            pltpu.VMEM((rows, buses), jnp.float32),
            pltpu.SemaphoreType.DMA((CHUNKS + 1,)),
        ],
    )
    inverse = call(inverse_kernel, [(1, rows)], index, dtype=jnp.int32)
    flows = call(copy_kernel, [(hours, rows)], flows) + moved(flows, over_out[0])
    for move in over_out[1:]:
        flows = add_move(flows, move)
    flows, inverse, limits = lax.optimization_barrier((flows, inverse, limits))
    flow_out = call(select_kernel, [(hours, width)], flows, index)
    flow_out = flow_out + other_core(flow_out)
    flow_spread = call(spread_kernel, [(hours, rows, LANES)], flows, mib=16)
    flow_out, flow_spread = lax.optimization_barrier((flow_out, flow_spread))
    for move in over_line[:-1]:
        flow_out = add_move(flow_out, move)
    flow_out = add_move(flow_out, over_line[-1])
    parts = call(thirds_kernel, [(3, rows, buses)], transfer_factors, dtype=jnp.bfloat16, mib=16)
    flow_out, parts = lax.optimization_barrier((flow_out, parts))
    sums, column_part = call(
        overload_kernel,
        [(hours, rows, LANES), (hours, width)],
        outage_factors,
        flow_spread,
        limits,
        flow_out,
        mib=24,
        scratch=[
            pltpu.VMEM((hours * blocks, SUB, LANES), jnp.float32),
            pltpu.VMEM((hours * blocks, SUB, LANES), jnp.float32),
        ],
    )
    column_total = column_part + other_core(column_part)
    row_part = call(row_kernel, [(hours, rows)], sums, mib=16)
    column_total, row_part = lax.optimization_barrier((column_total, row_part))
    copies = jnp.broadcast_to(column_total, (lines // 2,) + column_total.shape)
    column_total = lax.all_to_all(
        copies, "line", 0, 0, axis_index_groups=[list(range(c, lines, 2)) for c in range(2)], tiled=True
    ).sum(0)
    slopes = call(place_kernel, [(hours, rows)], column_total, inverse, row_part)
    for move in over_out:
        slopes = add_move(slopes, move)
    pieces = call(bus_kernel, [(lines, hours, LANES)], slopes, parts, mib=16)
    gradient = lax.all_to_all(pieces, "line", 0, 0, tiled=True).sum(0)
    return gradient[:, : buses // lines]


def solution(mesh):
    in_specs = (P(None, "out"), P("line", "out"), P("line", "out"), P("line"), P())
    out_specs = P(None, ("out", "line"))
    return jax.shard_map(local, mesh=mesh, in_specs=in_specs, out_specs=out_specs, check_vma=False)
```

```python
import functools

import jax
import jax.numpy as jnp
from jax import lax
from jax.experimental import pallas as pl
from jax.experimental.pallas import tpu as pltpu
from jax.sharding import PartitionSpec as P

OUTAGES = 16384
SOFTNESS = 0.25
LANES = 128
SUB = 8
TILES = 4
CHUNKS = 2
VMEM = pl.BlockSpec(memory_space=pltpu.VMEM)
FAR = pl.BlockSpec(memory_space=pltpu.HBM)


def params(mib):
    return pltpu.CompilerParams(vmem_limit_bytes=mib * 1024 * 1024)


def thirds(x):
    high = x.astype(jnp.bfloat16)
    rest = x - high.astype(jnp.float32)
    middle = rest.astype(jnp.bfloat16)
    return high, middle, (rest - middle.astype(jnp.float32)).astype(jnp.bfloat16)


def stacked(x):
    parts = [part.astype(jnp.float32) for part in thirds(x)]
    return jnp.concatenate(parts + [jnp.zeros_like(x)], axis=0).astype(jnp.bfloat16)


def product(parts, right, dims):
    first, second, third = (
        lax.dot_general(parts, part, dims, preferred_element_type=jnp.float32) for part in right
    )
    h = parts.shape[0] // 4
    small = first[2 * h : 3 * h] + second[h : 2 * h] + third[:h]
    return (small + (first[h : 2 * h] + second[:h])) + first[:h]


def flows_kernel(injections_hbm, factors_hbm, out_ref, injections, factors, sems):
    chunks = sems.shape[0] - 1
    rows = factors.shape[0] // chunks
    first = pltpu.make_async_copy(injections_hbm, injections, sems.at[chunks])
    first.start()
    copies = []
    for c in range(chunks):
        here = pl.ds(c * rows, rows)
        copies.append(pltpu.make_async_copy(factors_hbm.at[here, :], factors.at[here, :], sems.at[c]))
        copies[c].start()
    first.wait()
    parts = stacked(injections[...])
    for c in range(chunks):
        copies[c].wait()
        here = slice(c * rows, (c + 1) * rows)
        out_ref[:, here] = product(parts, thirds(factors[here, :]), (((1,), (1,)), ((), ())))


def copy_kernel(x_ref, out_ref):
    out_ref[...] = x_ref[...]


def thirds_kernel(x_ref, out_ref):
    for part, third in enumerate(thirds(x_ref[...])):
        out_ref[part] = third


def bus_kernel(slopes_ref, factors_ref, out_ref):
    parts = [factors_ref[part] for part in range(factors_ref.shape[0])]
    terms = product(stacked(slopes_ref[...]), parts, (((1,), (0,)), ((), ())))
    pieces, hours, lanes = out_ref.shape
    own = terms.shape[1] // pieces
    out_ref[...] = jnp.zeros_like(out_ref)
    for p in range(pieces):
        out_ref[p, :, :own] = terms[:, p * own : (p + 1) * own]


def inverse_kernel(index_ref, limit_ref, out_ref, limit_out_ref):
    for lb in range(limit_out_ref.shape[0] // LANES):
        here = slice(lb * LANES, (lb + 1) * LANES)
        limit = (0.5 / SOFTNESS) * limit_ref[:, here]
        limit_out_ref[here, :] = jnp.transpose(jnp.broadcast_to(limit, (LANES, LANES)))
    width = index_ref.shape[1]
    lane = lax.broadcasted_iota(jnp.int32, (LANES, LANES), 1)
    row = lax.broadcasted_iota(jnp.int32, (LANES, LANES), 0)
    totals = [jnp.zeros((1, LANES), jnp.int32) for _ in range(out_ref.shape[1] // LANES)]
    for kb in range(width // LANES):
        piece = index_ref[:, kb * LANES : (kb + 1) * LANES].astype(jnp.float32)
        column = jnp.transpose(jnp.broadcast_to(piece, (LANES, LANES))).astype(jnp.int32)
        for lb in range(len(totals)):
            hit = jnp.where(column == lane + lb * LANES, row + (kb * LANES + 1), 0)
            totals[lb] = totals[lb] + jnp.sum(hit, axis=0, keepdims=True)
    for lb, total in enumerate(totals):
        out_ref[:, lb * LANES : (lb + 1) * LANES] = total - 1


def pick(values_ref, index_ref, kb):
    hours, width = values_ref.shape
    index = jnp.broadcast_to(index_ref[:, kb * LANES : (kb + 1) * LANES], (hours, LANES))
    low = jnp.bitwise_and(index, LANES - 1)
    high = jnp.right_shift(index, 7)
    result = jnp.zeros((hours, LANES), jnp.float32)
    for q in range(width // LANES):
        found = jnp.take_along_axis(values_ref[:, q * LANES : (q + 1) * LANES], low, axis=1)
        result = jnp.where(high == q, found, result)
    return result


def select_kernel(values_ref, index_ref, out_ref):
    for kb in range(out_ref.shape[1] // LANES):
        out_ref[:, kb * LANES : (kb + 1) * LANES] = pick(values_ref, index_ref, kb)


def place_kernel(values_ref, index_ref, rows_ref, out_ref):
    for kb in range(out_ref.shape[1] // LANES):
        here = slice(kb * LANES, (kb + 1) * LANES)
        out_ref[:, here] = pick(values_ref, index_ref, kb) + rows_ref[:, here]


def spread_kernel(flow_ref, out_ref):
    hours, rows = flow_ref.shape
    for h in range(hours):
        for lb in range(rows // LANES):
            here = slice(lb * LANES, (lb + 1) * LANES)
            flow = (0.5 / SOFTNESS) * flow_ref[h : h + 1, here]
            out_ref[h, here, :] = jnp.transpose(jnp.broadcast_to(flow, (LANES, LANES)))


def overload_kernel(
    factors_ref, flow_ref, limit_ref, out_flow_ref, sums_ref, column_ref, wide, total
):
    rows, width = factors_ref.shape
    hours = flow_ref.shape[0]
    blocks = width // LANES
    parts = range(TILES)
    tile = TILES * SUB
    for h in range(hours):
        for kb in range(blocks):
            piece = (0.5 / SOFTNESS) * out_flow_ref[h : h + 1, kb * LANES : (kb + 1) * LANES]
            wide[h * blocks + kb] = jnp.broadcast_to(piece, (SUB, LANES))
    total[...] = jnp.zeros_like(total)

    def advance(step, carry):
        start = pl.multiple_of(step * tile, tile)
        at = [pl.ds(start + r * SUB, SUB) for r in parts]
        limit = [limit_ref[at[r], :] for r in parts]
        for h in range(hours):
            flow = [flow_ref[h, at[r], :] for r in parts]
            plus = [flow[r] + limit[r] for r in parts]
            minus = [flow[r] - limit[r] for r in parts]
            across = [None for r in parts]
            for kb in range(blocks):
                out_flow = wide[h * blocks + kb]
                gathered = None
                for r in parts:
                    factor = factors_ref[at[r], kb * LANES : (kb + 1) * LANES]
                    moved = factor * out_flow
                    slope = jnp.tanh(moved + plus[r]) + jnp.tanh(moved + minus[r])
                    across[r] = slope if across[r] is None else across[r] + slope
                    weighted = slope * factor
                    gathered = weighted if gathered is None else gathered + weighted
                total[h * blocks + kb] = total[h * blocks + kb] + gathered
            for r in parts:
                sums_ref[h, at[r], :] = across[r]
        return carry

    lax.fori_loop(0, rows // tile, advance, 0)
    for h in range(hours):
        for kb in range(blocks):
            column_ref[h : h + 1, kb * LANES : (kb + 1) * LANES] = (0.5 / OUTAGES) * jnp.sum(
                total[h * blocks + kb], axis=0, keepdims=True
            )


def row_kernel(sums_ref, out_ref):
    hours, rows = out_ref.shape
    for lb in range(rows // LANES):
        here = slice(lb * LANES, (lb + 1) * LANES)
        for h in range(hours):
            out_ref[h : h + 1, here] = (0.5 / OUTAGES) * jnp.sum(
                jnp.transpose(sums_ref[h, here, :]), axis=0, keepdims=True
            )


def call(kernel, shape, *operands, dtype=jnp.float32, mib=8, far=0, scratch=()):
    size = sum(a.size * 4 for a in operands)
    kinds = dtype if isinstance(dtype, tuple) else [dtype] * len(shape)
    out_shape = [jax.ShapeDtypeStruct(s, kind) for s, kind in zip(shape, kinds)]
    result = pl.pallas_call(
        kernel,
        out_shape=out_shape,
        in_specs=[FAR] * far + [VMEM] * (len(operands) - far),
        out_specs=[VMEM] * len(shape),
        scratch_shapes=list(scratch),
        compiler_params=params(mib),
        cost_estimate=pl.CostEstimate(flops=0, bytes_accessed=size, transcendentals=0),
        name=kernel.__name__,
    )(*operands)
    return result[0] if len(shape) == 1 else result


def pairs_over(dims, moves):
    lines, outs = dims
    pairs = []
    for i in range(lines):
        for o in range(outs):
            to_line, to_out = moves(i, o)
            pairs.append((i * outs + o, to_line * outs + to_out))
    return pairs


def out_moves(outs):
    depth = outs // 2
    moves = [lambda i, o: (i, o ^ depth)]
    bit = 1
    while bit < depth // 2:
        moves.append(lambda i, o, bit=bit: (i, o ^ bit))
        bit *= 2
    if depth > 1:
        moves.append(lambda i, o: (i, (o & depth) | (depth - 1 - (o & (depth - 1)))))
    return moves


def line_moves(lines):
    half = lines // 2
    moves = [lambda i, o: (i ^ half ^ 1, o)]
    if half > 2:
        moves.append(lambda i, o: (i ^ (half - 2) ^ 1, o))
    bit = 2
    while bit < half // 2:
        moves.append(lambda i, o, bit=bit: (i ^ bit ^ 1, o))
        bit *= 2
    return moves


def local(injections, transfer_factors, outage_factors, line_limits, outage_lines):
    rows, buses = transfer_factors.shape
    hours = injections.shape[0]
    width = outage_factors.shape[1]
    blocks = width // LANES
    lines, outs = lax.axis_size("line"), lax.axis_size("out")
    line = lax.axis_index("line")
    out_start = lax.axis_index("out") * width
    index = lax.dynamic_slice_in_dim(outage_lines, out_start, width, 0) - line * rows
    index = index.reshape(1, width)

    def moved(x, move):
        return lax.ppermute(x, ("line", "out"), pairs_over((lines, outs), move))

    def add_move(x, move):
        return x + moved(x, move)

    def other_core(x):
        return lax.ppermute(x, "line", [(i, i ^ 1) for i in range(lines)])

    over_out, over_line = out_moves(outs), line_moves(lines)
    flows = call(
        flows_kernel,
        [(hours, rows)],
        injections,
        transfer_factors,
        mib=60,
        far=2,
        scratch=[
            pltpu.VMEM((hours, buses), jnp.float32),
            pltpu.VMEM((rows, buses), jnp.float32),
            pltpu.SemaphoreType.DMA((CHUNKS + 1,)),
        ],
    )
    inverse, limits = call(
        inverse_kernel,
        [(1, rows), (rows, LANES)],
        index,
        line_limits.reshape(1, rows),
        dtype=(jnp.int32, jnp.float32),
    )
    flows = call(copy_kernel, [(hours, rows)], flows) + moved(flows, over_out[0])
    for move in over_out[1:]:
        flows = add_move(flows, move)
    flows, inverse, limits = lax.optimization_barrier((flows, inverse, limits))
    flow_out = call(select_kernel, [(hours, width)], flows, index)
    flow_out = flow_out + other_core(flow_out)
    flow_spread = call(spread_kernel, [(hours, rows, LANES)], flows, mib=16)
    flow_out, flow_spread = lax.optimization_barrier((flow_out, flow_spread))
    for move in over_line[:-1]:
        flow_out = add_move(flow_out, move)
    flow_out = add_move(flow_out, over_line[-1])
    parts = call(thirds_kernel, [(3, rows, buses)], transfer_factors, dtype=jnp.bfloat16, mib=16)
    flow_out, parts = lax.optimization_barrier((flow_out, parts))
    sums, column_part = call(
        overload_kernel,
        [(hours, rows, LANES), (hours, width)],
        outage_factors,
        flow_spread,
        limits,
        flow_out,
        mib=24,
        scratch=[
            pltpu.VMEM((hours * blocks, SUB, LANES), jnp.float32),
            pltpu.VMEM((hours * blocks, SUB, LANES), jnp.float32),
        ],
    )
    column_total = column_part + other_core(column_part)
    row_part = call(row_kernel, [(hours, rows)], sums, mib=16)
    column_total, row_part = lax.optimization_barrier((column_total, row_part))
    copies = jnp.broadcast_to(column_total, (lines // 2,) + column_total.shape)
    column_total = lax.all_to_all(
        copies, "line", 0, 0, axis_index_groups=[list(range(c, lines, 2)) for c in range(2)], tiled=True
    ).sum(0)
    slopes = call(place_kernel, [(hours, rows)], column_total, inverse, row_part)
    for move in over_out:
        slopes = add_move(slopes, move)
    pieces = call(bus_kernel, [(lines, hours, LANES)], slopes, parts, mib=16)
    gradient = lax.all_to_all(pieces, "line", 0, 0, tiled=True).sum(0)
    return gradient[:, : buses // lines]


def solution(mesh):
    in_specs = (P(None, "out"), P("line", "out"), P("line", "out"), P("line"), P())
    out_specs = P(None, ("out", "line"))
    return jax.shard_map(local, mesh=mesh, in_specs=in_specs, out_specs=out_specs, check_vma=False)
```

```python
import functools

import jax
import jax.numpy as jnp
from jax import lax
from jax.experimental import pallas as pl
from jax.experimental.pallas import tpu as pltpu
from jax.sharding import PartitionSpec as P

OUTAGES = 16384
SOFTNESS = 0.25
LANES = 128
SUB = 8
TILES = 4
CHUNKS = 2
VMEM = pl.BlockSpec(memory_space=pltpu.VMEM)
FAR = pl.BlockSpec(memory_space=pltpu.HBM)


def params(mib):
    return pltpu.CompilerParams(vmem_limit_bytes=mib * 1024 * 1024)


def thirds(x):
    high = x.astype(jnp.bfloat16)
    rest = x - high.astype(jnp.float32)
    middle = rest.astype(jnp.bfloat16)
    return high, middle, (rest - middle.astype(jnp.float32)).astype(jnp.bfloat16)


def stacked(x):
    parts = [part.astype(jnp.float32) for part in thirds(x)]
    return jnp.concatenate(parts + [jnp.zeros_like(x)], axis=0).astype(jnp.bfloat16)


def product(parts, right, dims):
    first, second, third = (
        lax.dot_general(parts, part, dims, preferred_element_type=jnp.float32) for part in right
    )
    h = parts.shape[0] // 4
    small = first[2 * h : 3 * h] + second[h : 2 * h] + third[:h]
    return (small + (first[h : 2 * h] + second[:h])) + first[:h]


def flows_kernel(injections_hbm, factors_hbm, out_ref, injections, factors, sems):
    chunks = sems.shape[0] - 1
    rows = factors.shape[0] // chunks
    first = pltpu.make_async_copy(injections_hbm, injections, sems.at[chunks])
    first.start()
    copies = []
    for c in range(chunks):
        here = pl.ds(c * rows, rows)
        copies.append(pltpu.make_async_copy(factors_hbm.at[here, :], factors.at[here, :], sems.at[c]))
        copies[c].start()
    first.wait()
    parts = stacked(injections[...])
    for c in range(chunks):
        copies[c].wait()
        here = slice(c * rows, (c + 1) * rows)
        out_ref[:, here] = product(parts, thirds(factors[here, :]), (((1,), (1,)), ((), ())))


def copy_kernel(x_ref, out_ref):
    out_ref[...] = x_ref[...]


def thirds_kernel(x_ref, out_ref):
    for part, third in enumerate(thirds(x_ref[...])):
        out_ref[part] = third


def bus_kernel(slopes_ref, factors_ref, out_ref):
    parts = [factors_ref[part] for part in range(factors_ref.shape[0])]
    terms = product(stacked(slopes_ref[...]), parts, (((1,), (0,)), ((), ())))
    pieces, hours, lanes = out_ref.shape
    own = terms.shape[1] // pieces
    out_ref[...] = jnp.zeros_like(out_ref)
    for p in range(pieces):
        out_ref[p, :, :own] = terms[:, p * own : (p + 1) * own]


def inverse_kernel(index_ref, limit_ref, out_ref, limit_out_ref):
    for lb in range(limit_out_ref.shape[0] // LANES):
        here = slice(lb * LANES, (lb + 1) * LANES)
        limit = (0.5 / SOFTNESS) * limit_ref[:, here]
        limit_out_ref[here, :] = jnp.transpose(jnp.broadcast_to(limit, (LANES, LANES)))
    width = index_ref.shape[1]
    lane = lax.broadcasted_iota(jnp.int32, (LANES, LANES), 1)
    row = lax.broadcasted_iota(jnp.int32, (LANES, LANES), 0)
    totals = [jnp.zeros((1, LANES), jnp.int32) for _ in range(out_ref.shape[1] // LANES)]
    for kb in range(width // LANES):
        piece = index_ref[:, kb * LANES : (kb + 1) * LANES].astype(jnp.float32)
        column = jnp.transpose(jnp.broadcast_to(piece, (LANES, LANES))).astype(jnp.int32)
        for lb in range(len(totals)):
            hit = jnp.where(column == lane + lb * LANES, row + (kb * LANES + 1), 0)
            totals[lb] = totals[lb] + jnp.sum(hit, axis=0, keepdims=True)
    for lb, total in enumerate(totals):
        out_ref[:, lb * LANES : (lb + 1) * LANES] = total - 1


def pick(values_ref, index_ref, kb):
    hours, width = values_ref.shape
    index = jnp.broadcast_to(index_ref[:, kb * LANES : (kb + 1) * LANES], (hours, LANES))
    low = jnp.bitwise_and(index, LANES - 1)
    high = jnp.right_shift(index, 7)
    result = jnp.zeros((hours, LANES), jnp.float32)
    for q in range(width // LANES):
        found = jnp.take_along_axis(values_ref[:, q * LANES : (q + 1) * LANES], low, axis=1)
        result = jnp.where(high == q, found, result)
    return result


def select_kernel(values_ref, index_ref, out_ref):
    for kb in range(out_ref.shape[1] // LANES):
        out_ref[:, kb * LANES : (kb + 1) * LANES] = pick(values_ref, index_ref, kb)


def place_kernel(values_ref, index_ref, rows_ref, out_ref):
    for kb in range(out_ref.shape[1] // LANES):
        here = slice(kb * LANES, (kb + 1) * LANES)
        out_ref[:, here] = pick(values_ref, index_ref, kb) + rows_ref[:, here]


def spread_kernel(flow_ref, out_ref):
    hours, rows = flow_ref.shape
    for h in range(hours):
        for lb in range(rows // LANES):
            here = slice(lb * LANES, (lb + 1) * LANES)
            flow = (0.5 / SOFTNESS) * flow_ref[h : h + 1, here]
            out_ref[h, here, :] = jnp.transpose(jnp.broadcast_to(flow, (LANES, LANES)))


def overload_kernel(
    factors_ref, flow_ref, limit_ref, out_flow_ref, sums_ref, column_ref, wide, total
):
    rows, width = factors_ref.shape
    hours = flow_ref.shape[0]
    blocks = width // LANES
    parts = range(TILES)
    tile = TILES * SUB
    wide[...] = (0.5 / SOFTNESS) * out_flow_ref[...]
    total[...] = jnp.zeros_like(total)

    def advance(step, carry):
        start = pl.multiple_of(step * tile, tile)
        at = [pl.ds(start + r * SUB, SUB) for r in parts]
        limit = [limit_ref[at[r], :] for r in parts]
        for h in range(hours):
            flow = [flow_ref[h, at[r], :] for r in parts]
            plus = [flow[r] + limit[r] for r in parts]
            minus = [flow[r] - limit[r] for r in parts]
            across = [None for r in parts]
            for kb in range(blocks):
                out_flow = wide[h : h + 1, kb * LANES : (kb + 1) * LANES]
                gathered = None
                for r in parts:
                    factor = factors_ref[at[r], kb * LANES : (kb + 1) * LANES]
                    moved = factor * out_flow
                    slope = jnp.tanh(moved + plus[r]) + jnp.tanh(moved + minus[r])
                    across[r] = slope if across[r] is None else across[r] + slope
                    weighted = slope * factor
                    gathered = weighted if gathered is None else gathered + weighted
                total[h * blocks + kb] = total[h * blocks + kb] + gathered
            for r in parts:
                sums_ref[h, at[r], :] = across[r]
        return carry

    lax.fori_loop(0, rows // tile, advance, 0)
    for h in range(hours):
        for kb in range(blocks):
            column_ref[h : h + 1, kb * LANES : (kb + 1) * LANES] = (0.5 / OUTAGES) * jnp.sum(
                total[h * blocks + kb], axis=0, keepdims=True
            )


def row_kernel(sums_ref, out_ref):
    hours, rows = out_ref.shape
    for lb in range(rows // LANES):
        here = slice(lb * LANES, (lb + 1) * LANES)
        for h in range(hours):
            out_ref[h : h + 1, here] = (0.5 / OUTAGES) * jnp.sum(
                jnp.transpose(sums_ref[h, here, :]), axis=0, keepdims=True
            )


def call(kernel, shape, *operands, dtype=jnp.float32, mib=8, far=0, scratch=()):
    size = sum(a.size * 4 for a in operands)
    kinds = dtype if isinstance(dtype, tuple) else [dtype] * len(shape)
    out_shape = [jax.ShapeDtypeStruct(s, kind) for s, kind in zip(shape, kinds)]
    result = pl.pallas_call(
        kernel,
        out_shape=out_shape,
        in_specs=[FAR] * far + [VMEM] * (len(operands) - far),
        out_specs=[VMEM] * len(shape),
        scratch_shapes=list(scratch),
        compiler_params=params(mib),
        cost_estimate=pl.CostEstimate(flops=0, bytes_accessed=size, transcendentals=0),
        name=kernel.__name__,
    )(*operands)
    return result[0] if len(shape) == 1 else result


def pairs_over(dims, moves):
    lines, outs = dims
    pairs = []
    for i in range(lines):
        for o in range(outs):
            to_line, to_out = moves(i, o)
            pairs.append((i * outs + o, to_line * outs + to_out))
    return pairs


def out_moves(outs):
    depth = outs // 2
    moves = [lambda i, o: (i, o ^ depth)]
    bit = 1
    while bit < depth // 2:
        moves.append(lambda i, o, bit=bit: (i, o ^ bit))
        bit *= 2
    if depth > 1:
        moves.append(lambda i, o: (i, (o & depth) | (depth - 1 - (o & (depth - 1)))))
    return moves


def line_moves(lines):
    half = lines // 2
    moves = [lambda i, o: (i ^ half ^ 1, o)]
    if half > 2:
        moves.append(lambda i, o: (i ^ (half - 2) ^ 1, o))
    bit = 2
    while bit < half // 2:
        moves.append(lambda i, o, bit=bit: (i ^ bit ^ 1, o))
        bit *= 2
    return moves


def local(injections, transfer_factors, outage_factors, line_limits, outage_lines):
    rows, buses = transfer_factors.shape
    hours = injections.shape[0]
    width = outage_factors.shape[1]
    blocks = width // LANES
    lines, outs = lax.axis_size("line"), lax.axis_size("out")
    line = lax.axis_index("line")
    out_start = lax.axis_index("out") * width
    index = lax.dynamic_slice_in_dim(outage_lines, out_start, width, 0) - line * rows
    index = index.reshape(1, width)

    def moved(x, move):
        return lax.ppermute(x, ("line", "out"), pairs_over((lines, outs), move))

    def add_move(x, move):
        return x + moved(x, move)

    def other_core(x):
        return lax.ppermute(x, "line", [(i, i ^ 1) for i in range(lines)])

    over_out, over_line = out_moves(outs), line_moves(lines)
    flows = call(
        flows_kernel,
        [(hours, rows)],
        injections,
        transfer_factors,
        mib=60,
        far=2,
        scratch=[
            pltpu.VMEM((hours, buses), jnp.float32),
            pltpu.VMEM((rows, buses), jnp.float32),
            pltpu.SemaphoreType.DMA((CHUNKS + 1,)),
        ],
    )
    inverse, limits = call(
        inverse_kernel,
        [(1, rows), (rows, LANES)],
        index,
        line_limits.reshape(1, rows),
        dtype=(jnp.int32, jnp.float32),
    )
    back = over_out[::-1]
    flows = call(copy_kernel, [(hours, rows)], flows) + moved(flows, back[0])
    for move in back[1:]:
        flows = add_move(flows, move)
    flows, inverse, limits = lax.optimization_barrier((flows, inverse, limits))
    flow_out = call(select_kernel, [(hours, width)], flows, index)
    flow_out = flow_out + other_core(flow_out)
    flow_spread = call(spread_kernel, [(hours, rows, LANES)], flows, mib=16)
    flow_out, flow_spread = lax.optimization_barrier((flow_out, flow_spread))
    for move in over_line[:-1]:
        flow_out = add_move(flow_out, move)
    flow_out = add_move(flow_out, over_line[-1])
    parts = call(thirds_kernel, [(3, rows, buses)], transfer_factors, dtype=jnp.bfloat16, mib=16)
    flow_out, parts = lax.optimization_barrier((flow_out, parts))
    sums, column_part = call(
        overload_kernel,
        [(hours, rows, LANES), (hours, width)],
        outage_factors,
        flow_spread,
        limits,
        flow_out,
        mib=24,
        scratch=[
            pltpu.VMEM((hours, width), jnp.float32),
            pltpu.VMEM((hours * blocks, SUB, LANES), jnp.float32),
        ],
    )
    column_total = column_part + other_core(column_part)
    row_part = call(row_kernel, [(hours, rows)], sums, mib=16)
    column_total, row_part = lax.optimization_barrier((column_total, row_part))
    copies = jnp.broadcast_to(column_total, (lines // 2,) + column_total.shape)
    column_total = lax.all_to_all(
        copies, "line", 0, 0, axis_index_groups=[list(range(c, lines, 2)) for c in range(2)], tiled=True
    ).sum(0)
    slopes = call(place_kernel, [(hours, rows)], column_total, inverse, row_part)
    for move in over_out:
        slopes = add_move(slopes, move)
    pieces = call(bus_kernel, [(lines, hours, LANES)], slopes, parts, mib=16)
    gradient = lax.all_to_all(pieces, "line", 0, 0, tiled=True).sum(0)
    return gradient[:, : buses // lines]


def solution(mesh):
    in_specs = (P(None, "out"), P("line", "out"), P("line", "out"), P("line"), P())
    out_specs = P(None, ("out", "line"))
    return jax.shard_map(local, mesh=mesh, in_specs=in_specs, out_specs=out_specs, check_vma=False)
```

```python
import functools

import jax
import jax.numpy as jnp
from jax import lax
from jax.experimental import pallas as pl
from jax.experimental.pallas import tpu as pltpu
from jax.sharding import PartitionSpec as P

OUTAGES = 16384
SOFTNESS = 0.25
LANES = 128
SUB = 8
TILES = 4
CHUNKS = 2
VMEM = pl.BlockSpec(memory_space=pltpu.VMEM)
FAR = pl.BlockSpec(memory_space=pltpu.HBM)


def params(mib):
    return pltpu.CompilerParams(vmem_limit_bytes=mib * 1024 * 1024)


def thirds(x):
    high = x.astype(jnp.bfloat16)
    rest = x - high.astype(jnp.float32)
    middle = rest.astype(jnp.bfloat16)
    return high, middle, (rest - middle.astype(jnp.float32)).astype(jnp.bfloat16)


def stacked(x):
    parts = [part.astype(jnp.float32) for part in thirds(x)]
    return jnp.concatenate(parts + [jnp.zeros_like(x)], axis=0).astype(jnp.bfloat16)


def product(parts, right, dims):
    first, second, third = (
        lax.dot_general(parts, part, dims, preferred_element_type=jnp.float32) for part in right
    )
    h = parts.shape[0] // 4
    small = first[2 * h : 3 * h] + second[h : 2 * h] + third[:h]
    return (small + (first[h : 2 * h] + second[:h])) + first[:h]


def flows_kernel(injections_hbm, factors_hbm, out_ref, injections, factors, sems):
    chunks = sems.shape[0] - 1
    rows = factors.shape[0] // chunks
    first = pltpu.make_async_copy(injections_hbm, injections, sems.at[chunks])
    first.start()
    copies = []
    for c in range(chunks):
        here = pl.ds(c * rows, rows)
        copies.append(pltpu.make_async_copy(factors_hbm.at[here, :], factors.at[here, :], sems.at[c]))
        copies[c].start()
    first.wait()
    parts = stacked(injections[...])
    for c in range(chunks):
        copies[c].wait()
        here = slice(c * rows, (c + 1) * rows)
        out_ref[:, here] = product(parts, thirds(factors[here, :]), (((1,), (1,)), ((), ())))


def copy_kernel(x_ref, out_ref):
    out_ref[...] = x_ref[...]


def thirds_kernel(x_ref, out_ref):
    for part, third in enumerate(thirds(x_ref[...])):
        out_ref[part] = third


def bus_kernel(slopes_ref, factors_ref, out_ref):
    parts = [factors_ref[part] for part in range(factors_ref.shape[0])]
    terms = product(stacked(slopes_ref[...]), parts, (((1,), (0,)), ((), ())))
    pieces, hours, lanes = out_ref.shape
    own = terms.shape[1] // pieces
    out_ref[...] = jnp.zeros_like(out_ref)
    for p in range(pieces):
        out_ref[p, :, :own] = terms[:, p * own : (p + 1) * own]


def inverse_kernel(index_ref, limit_ref, out_ref, limit_out_ref):
    for lb in range(limit_out_ref.shape[0] // LANES):
        here = slice(lb * LANES, (lb + 1) * LANES)
        limit = (0.5 / SOFTNESS) * limit_ref[:, here]
        limit_out_ref[here, :] = jnp.transpose(jnp.broadcast_to(limit, (LANES, LANES)))
    width = index_ref.shape[1]
    lane = lax.broadcasted_iota(jnp.int32, (LANES, LANES), 1)
    row = lax.broadcasted_iota(jnp.int32, (LANES, LANES), 0)
    totals = [jnp.zeros((1, LANES), jnp.int32) for _ in range(out_ref.shape[1] // LANES)]
    for kb in range(width // LANES):
        piece = index_ref[:, kb * LANES : (kb + 1) * LANES].astype(jnp.float32)
        column = jnp.transpose(jnp.broadcast_to(piece, (LANES, LANES))).astype(jnp.int32)
        for lb in range(len(totals)):
            hit = jnp.where(column == lane + lb * LANES, row + (kb * LANES + 1), 0)
            totals[lb] = totals[lb] + jnp.sum(hit, axis=0, keepdims=True)
    for lb, total in enumerate(totals):
        out_ref[:, lb * LANES : (lb + 1) * LANES] = total - 1


def pick(values_ref, index_ref, kb):
    hours, width = values_ref.shape
    index = jnp.broadcast_to(index_ref[:, kb * LANES : (kb + 1) * LANES], (hours, LANES))
    low = jnp.bitwise_and(index, LANES - 1)
    high = jnp.right_shift(index, 7)
    result = jnp.zeros((hours, LANES), jnp.float32)
    for q in range(width // LANES):
        found = jnp.take_along_axis(values_ref[:, q * LANES : (q + 1) * LANES], low, axis=1)
        result = jnp.where(high == q, found, result)
    return result


def select_kernel(values_ref, index_ref, out_ref):
    for kb in range(out_ref.shape[1] // LANES):
        out_ref[:, kb * LANES : (kb + 1) * LANES] = pick(values_ref, index_ref, kb)


def place_kernel(values_ref, index_ref, rows_ref, out_ref):
    for kb in range(out_ref.shape[1] // LANES):
        here = slice(kb * LANES, (kb + 1) * LANES)
        out_ref[:, here] = pick(values_ref, index_ref, kb) + rows_ref[:, here]


def spread_kernel(flow_ref, out_ref):
    hours, rows = flow_ref.shape
    for h in range(hours):
        for lb in range(rows // LANES):
            here = slice(lb * LANES, (lb + 1) * LANES)
            flow = (0.5 / SOFTNESS) * flow_ref[h : h + 1, here]
            out_ref[h, here, :] = jnp.transpose(jnp.broadcast_to(flow, (LANES, LANES)))


def overload_kernel(
    factors_ref, flow_ref, limit_ref, out_flow_ref, sums_ref, column_ref, wide, total
):
    rows, width = factors_ref.shape
    hours = flow_ref.shape[0]
    blocks = width // LANES
    parts = range(TILES)
    tile = TILES * SUB
    wide[...] = (0.5 / SOFTNESS) * out_flow_ref[...]
    total[...] = jnp.zeros_like(total)

    def advance(step, carry):
        start = pl.multiple_of(step * tile, tile)
        at = [pl.ds(start + r * SUB, SUB) for r in parts]
        limit = [limit_ref[at[r], :] for r in parts]
        for h in range(hours):
            flow = [flow_ref[h, at[r], :] for r in parts]
            plus = [flow[r] + limit[r] for r in parts]
            minus = [flow[r] - limit[r] for r in parts]
            across = [None for r in parts]
            for kb in range(blocks):
                out_flow = wide[h : h + 1, kb * LANES : (kb + 1) * LANES]
                gathered = None
                for r in parts:
                    factor = factors_ref[at[r], kb * LANES : (kb + 1) * LANES]
                    moved = factor * out_flow
                    slope = jnp.tanh(moved + plus[r]) + jnp.tanh(moved + minus[r])
                    across[r] = slope if across[r] is None else across[r] + slope
                    weighted = slope * factor
                    gathered = weighted if gathered is None else gathered + weighted
                total[h * blocks + kb] = total[h * blocks + kb] + gathered
            for r in parts:
                sums_ref[h, at[r], :] = across[r]
        return carry

    lax.fori_loop(0, rows // tile, advance, 0)
    for h in range(hours):
        for kb in range(blocks):
            column_ref[h : h + 1, kb * LANES : (kb + 1) * LANES] = (0.5 / OUTAGES) * jnp.sum(
                total[h * blocks + kb], axis=0, keepdims=True
            )


def row_kernel(sums_ref, out_ref):
    hours, rows = out_ref.shape
    for lb in range(rows // LANES):
        here = slice(lb * LANES, (lb + 1) * LANES)
        for h in range(hours):
            out_ref[h : h + 1, here] = (0.5 / OUTAGES) * jnp.sum(
                jnp.transpose(sums_ref[h, here, :]), axis=0, keepdims=True
            )


def call(kernel, shape, *operands, dtype=jnp.float32, mib=8, far=0, scratch=()):
    size = sum(a.size * 4 for a in operands)
    kinds = dtype if isinstance(dtype, tuple) else [dtype] * len(shape)
    out_shape = [jax.ShapeDtypeStruct(s, kind) for s, kind in zip(shape, kinds)]
    result = pl.pallas_call(
        kernel,
        out_shape=out_shape,
        in_specs=[FAR] * far + [VMEM] * (len(operands) - far),
        out_specs=[VMEM] * len(shape),
        scratch_shapes=list(scratch),
        compiler_params=params(mib),
        cost_estimate=pl.CostEstimate(flops=0, bytes_accessed=size, transcendentals=0),
        name=kernel.__name__,
    )(*operands)
    return result[0] if len(shape) == 1 else result


def pairs_over(dims, moves):
    lines, outs = dims
    pairs = []
    for i in range(lines):
        for o in range(outs):
            to_line, to_out = moves(i, o)
            pairs.append((i * outs + o, to_line * outs + to_out))
    return pairs


def out_moves(outs):
    depth = outs // 2
    moves = [lambda i, o: (i, o ^ depth)]
    bit = 1
    while bit < depth // 2:
        moves.append(lambda i, o, bit=bit: (i, o ^ bit))
        bit *= 2
    if depth > 1:
        moves.append(lambda i, o: (i, (o & depth) | (depth - 1 - (o & (depth - 1)))))
    return moves


def line_moves(lines):
    half = lines // 2
    moves = [lambda i, o: (i ^ half ^ 1, o)]
    if half > 2:
        moves.append(lambda i, o: (i ^ (half - 2) ^ 1, o))
    bit = 2
    while bit < half // 2:
        moves.append(lambda i, o, bit=bit: (i ^ bit ^ 1, o))
        bit *= 2
    return moves


def local(injections, transfer_factors, outage_factors, line_limits, outage_lines):
    rows, buses = transfer_factors.shape
    hours = injections.shape[0]
    width = outage_factors.shape[1]
    blocks = width // LANES
    lines, outs = lax.axis_size("line"), lax.axis_size("out")
    line = lax.axis_index("line")
    out_start = lax.axis_index("out") * width
    index = lax.dynamic_slice_in_dim(outage_lines, out_start, width, 0) - line * rows
    index = index.reshape(1, width)

    def moved(x, move):
        return lax.ppermute(x, ("line", "out"), pairs_over((lines, outs), move))

    def add_move(x, move):
        return x + moved(x, move)

    def other_core(x):
        return lax.ppermute(x, "line", [(i, i ^ 1) for i in range(lines)])

    over_out, over_line = out_moves(outs), line_moves(lines)
    over_line = [over_line[1], over_line[0], *over_line[2:]]
    flows = call(
        flows_kernel,
        [(hours, rows)],
        injections,
        transfer_factors,
        mib=60,
        far=2,
        scratch=[
            pltpu.VMEM((hours, buses), jnp.float32),
            pltpu.VMEM((rows, buses), jnp.float32),
            pltpu.SemaphoreType.DMA((CHUNKS + 1,)),
        ],
    )
    inverse, limits = call(
        inverse_kernel,
        [(1, rows), (rows, LANES)],
        index,
        line_limits.reshape(1, rows),
        dtype=(jnp.int32, jnp.float32),
    )
    back = over_out[::-1]
    flows = call(copy_kernel, [(hours, rows)], flows) + moved(flows, back[0])
    for move in back[1:]:
        flows = add_move(flows, move)
    flows, inverse, limits = lax.optimization_barrier((flows, inverse, limits))
    flow_out = call(select_kernel, [(hours, width)], flows, index)
    flow_out = flow_out + other_core(flow_out)
    flow_spread = call(spread_kernel, [(hours, rows, LANES)], flows, mib=16)
    flow_out, flow_spread = lax.optimization_barrier((flow_out, flow_spread))
    for move in over_line[:-1]:
        flow_out = add_move(flow_out, move)
    flow_out = add_move(flow_out, over_line[-1])
    parts = call(thirds_kernel, [(3, rows, buses)], transfer_factors, dtype=jnp.bfloat16, mib=16)
    flow_out, parts = lax.optimization_barrier((flow_out, parts))
    sums, column_part = call(
        overload_kernel,
        [(hours, rows, LANES), (hours, width)],
        outage_factors,
        flow_spread,
        limits,
        flow_out,
        mib=24,
        scratch=[
            pltpu.VMEM((hours, width), jnp.float32),
            pltpu.VMEM((hours * blocks, SUB, LANES), jnp.float32),
        ],
    )
    column_total = column_part + other_core(column_part)
    row_part = call(row_kernel, [(hours, rows)], sums, mib=16)
    column_total, row_part = lax.optimization_barrier((column_total, row_part))
    copies = jnp.broadcast_to(column_total, (lines // 2,) + column_total.shape)
    column_total = lax.all_to_all(
        copies, "line", 0, 0, axis_index_groups=[list(range(c, lines, 2)) for c in range(2)], tiled=True
    ).sum(0)
    slopes = call(place_kernel, [(hours, rows)], column_total, inverse, row_part)
    for move in over_out:
        slopes = add_move(slopes, move)
    pieces = call(bus_kernel, [(lines, hours, LANES)], slopes, parts, mib=16)
    gradient = lax.all_to_all(pieces, "line", 0, 0, tiled=True).sum(0)
    return gradient[:, : buses // lines]


def solution(mesh):
    in_specs = (P(None, "out"), P("line", "out"), P("line", "out"), P("line"), P())
    out_specs = P(None, ("out", "line"))
    return jax.shard_map(local, mesh=mesh, in_specs=in_specs, out_specs=out_specs, check_vma=False)
```
